32 devices in a mesh: gy: 4 (over z), gx: 8 (over y, x, core).
Axes of the slice: x: 2, y: 2, z: 4, core: 2. Of those that a mesh axis runs over, the one named last changes fastest.
Arguments:
- source_field: float32 [2, 1, 4096, 4096], P(None, None, 'gx', 'gy'), may hold values from -5 to 5
- receiver_field: float32 [2, 1, 4096, 4096], P(None, None, 'gx', 'gy'), may hold values from -5 to 5
- velocity_index: int32 [4, 4096, 4096], P(None, 'gx', 'gy'), may hold values from 0 to 63
- slowness: float32 [64], replicated, may hold values from 0.25 to 1
- freq_index: int32 [1], replicated, may hold values from 8 to 511
- root_modulus: float32 [1], replicated, may hold values from 0.9 to 1, as said below
- root_angle: float32 [1], replicated, may hold values from -3.140625 to 3.140625
Outputs:
- image: float32 [4, 4096, 4096], P(None, 'gx', 'gy')
- source_bottom: float32 [2, 1, 4096, 4096], P(None, None, 'gx', 'gy')
- receiver_top: float32 [2, 1, 4096, 4096], P(None, None, 'gx', 'gy')
The draws below stay inside these ranges and needn't reach their ends.
Inputs may be any that keep to these rules, and one draw needn't show every extreme that they name: `root_modulus`: each modulus lies strictly below 1.
All inputs are finite; a program needn't handle non-finite values.
Results may differ from the reference program's by a relative error of at most 0.0003.
Values sent between devices are 32-bit elements; how exact they have to be, the bound alone decides.
No kernel may reach another device: no remote copies, remote signals or barrier semaphores. Data moves between devices by JAX's collectives and lax.ppermute only.
A program may use at most 192 MiB of HBM per device.

```python
import math
import jax
import jax.numpy as jnp
from jax import lax

NX = 4096
NY = 4096
FREQS = 1
DEPTH = 4
NVEL = 64


def draw_wave(key):
    shape = (2, FREQS, NX, NY)
    return jnp.clip(jax.random.normal(key, shape, jnp.float32), -5.0, 5.0)


def draw_source_field(key, part):
    return draw_wave(jax.random.fold_in(key, 11))


def draw_receiver_field(key, part):
    return draw_wave(jax.random.fold_in(key, 23))


def draw_root_modulus(key, part):
    unit = jax.random.uniform(jax.random.fold_in(key, 37), (FREQS,), jnp.float32)
    low_end = math.log(16.0)
    high_end = math.log(4096.0)
    reach = jnp.exp(low_end + (high_end - low_end) * unit)
    return jnp.exp(-1.0 / reach)


def touch_ends(entries, rng, low, largest):
    longest = entries.shape.index(max(entries.shape))
    spots = []
    for shift in (0, 1):
        where = [jax.random.randint(jax.random.fold_in(rng, axis), (), 0, length) for axis, length in enumerate(entries.shape)]
        where[longest] = (where[longest] + shift) % entries.shape[longest]
        spots.append(tuple(where))
    return entries.at[spots[0]].set(low).at[spots[1]].set(largest)


def setup_inputs(seed: int = 0) -> dict:
    splits = jax.random.split(jax.random.key(seed), 8)
    return {
        "source_field": draw_source_field(jax.random.fold_in(splits[7], 71), 0),
        "receiver_field": draw_receiver_field(jax.random.fold_in(splits[7], 71), 0),
        "velocity_index": touch_ends(jax.random.randint(splits[2], (DEPTH, NX, NY), 0, NVEL), jax.random.fold_in(splits[2], 1), 0, NVEL - 1).astype(jnp.int32),
        "slowness": jnp.clip(jnp.exp(jax.random.uniform(splits[3], (NVEL,), jnp.float32, math.log(0.25), math.log(1.0))), 0.25, 1.0),
        "freq_index": jax.random.randint(splits[4], (FREQS,), 8, 512).astype(jnp.int32),
        "root_modulus": draw_root_modulus(jax.random.fold_in(splits[7], 71), 0),
        "root_angle": jnp.clip(jax.random.uniform(splits[6], (FREQS,), jnp.float32, -3.140625, 3.140625), -3.140625, 3.140625),
    }


PHASE_UNIT = 0.05


def line_recur(wave_re, wave_im, modulus, angle, line_dim, backward):
    root_re = (modulus * jnp.cos(angle))[:, None]
    root_im = (modulus * jnp.sin(angle))[:, None]
    moved_re = jnp.moveaxis(wave_re, line_dim, 0)
    moved_im = jnp.moveaxis(wave_im, line_dim, 0)
    zeros_row = jnp.zeros_like(moved_re[0])

    def advance(carry_set, inputs):
        prev_re, prev_im, last_re, last_im = carry_set
        cur_re, cur_im = inputs
        next_re = root_re * prev_re - root_im * prev_im + last_re - (root_re * cur_re + root_im * cur_im)
        next_im = root_re * prev_im + root_im * prev_re + last_im - (root_re * cur_im - root_im * cur_re)
        return (next_re, next_im, cur_re, cur_im), (next_re, next_im)

    start_set = (zeros_row, zeros_row, zeros_row, zeros_row)
    final_set, outputs = lax.scan(advance, start_set, (moved_re, moved_im), reverse=backward)
    return jnp.moveaxis(outputs[0], 0, line_dim), jnp.moveaxis(outputs[1], 0, line_dim)


def sweep_line(wave_re, wave_im, modulus, angle, line_dim):
    ahead_re, ahead_im = line_recur(wave_re, wave_im, modulus, angle, line_dim, False)
    return line_recur(ahead_re, ahead_im, modulus, angle, line_dim, True)


def reference(source_field, receiver_field, velocity_index, slowness, freq_index, root_modulus, root_angle):
    phase_rate = freq_index.astype(jnp.float32)[:, None, None] * PHASE_UNIT
    back_angle = -root_angle

    def rotation(level_index):
        slow_cell = slowness[velocity_index[level_index]]
        phase_arg = phase_rate * slow_cell[None]
        return jnp.cos(phase_arg), jnp.sin(phase_arg)

    src_re = source_field[0]
    src_im = source_field[1]
    source_levels = []
    for level_index in range(DEPTH):
        source_levels.append((src_re, src_im))
        src_re, src_im = sweep_line(src_re, src_im, root_modulus, root_angle, 1)
        src_re, src_im = sweep_line(src_re, src_im, root_modulus, root_angle, 2)
        cos_part, sin_part = rotation(level_index)
        src_re, src_im = src_re * cos_part - src_im * sin_part, src_re * sin_part + src_im * cos_part
    rec_re = receiver_field[0]
    rec_im = receiver_field[1]
    images = [None] * DEPTH
    for level_index in reversed(range(DEPTH)):
        cos_part, sin_part = rotation(level_index)
        rec_re, rec_im = rec_re * cos_part + rec_im * sin_part, rec_im * cos_part - rec_re * sin_part
        rec_re, rec_im = sweep_line(rec_re, rec_im, root_modulus, back_angle, 2)
        rec_re, rec_im = sweep_line(rec_re, rec_im, root_modulus, back_angle, 1)
        level_re, level_im = source_levels[level_index]
        images[level_index] = jnp.sum(level_re * rec_re + level_im * rec_im, axis=0)
    return jnp.stack(images), jnp.stack([src_re, src_im]), jnp.stack([rec_re, rec_im])
```

```python
import functools

import jax
import jax.numpy as jnp
import numpy as np
from jax import lax
from jax.experimental import pallas as pl
from jax.experimental.pallas import tpu as pltpu
from jax.sharding import PartitionSpec as P

PHASE_UNIT = 0.05
W = 128
F32 = jnp.float32
BF16 = jnp.bfloat16
HIGHEST = lax.Precision.HIGHEST
VMEM_LIMIT = 48 * 1024 * 1024


def complex_mul(a, b):
    return (a[0] * b[0] - a[1] * b[1], a[0] * b[1] + a[1] * b[0])


def root_powers(modulus, angle, exponent):
    k = exponent.astype(F32)
    coarse = jnp.round(angle * 512.0)
    fine = angle - coarse * (1.0 / 512.0)
    steps = k * coarse
    turns = jnp.round(steps * np.float32(1.0 / 512.0 / (2.0 * np.pi)))
    spin = (steps * (1.0 / 512.0) - turns * 6.28125) - turns * np.float32(2.0 * np.pi - 6.28125)
    spin = spin + k * fine
    magnitude = jnp.exp(jnp.log(modulus) * k)
    return (magnitude * jnp.cos(spin), magnitude * jnp.sin(spin))


def sweep_factors(modulus, angle):
    sin, cos = jnp.sin(angle), jnp.cos(angle)
    gap = (1.0 - modulus) * (1.0 + modulus)
    re, im = modulus * cos, modulus * sin
    den_re, den_im = gap + 2.0 * im * im, -2.0 * re * im
    den_sq = den_re * den_re + den_im * den_im
    inv = (den_re / den_sq, -den_im / den_sq)
    diag = (re * re - im * im + gap * gap * inv[0], -2.0 * re * im + gap * gap * inv[1])
    root_inv = (re / (modulus * modulus), -im / (modulus * modulus))
    off = complex_mul((0.0 * im, 2.0 * gap * im), complex_mul(root_inv, inv))
    end = (-gap * gap * inv[0], -gap * gap * inv[1])
    return diag, off, end


def real_rows(pair):
    re, im = pair
    rows, n = re.shape
    nb = n // W
    first = jnp.stack([re.reshape(rows, nb, W), -im.reshape(rows, nb, W)], axis=2)
    second = jnp.stack([im.reshape(rows, nb, W), re.reshape(rows, nb, W)], axis=2)
    return jnp.stack([first, second], axis=1).reshape(2 * rows, 2 * n)


def spread_rows(pair):
    re, im = pair
    rows, n = re.shape
    nb = n // W
    first = jnp.stack([re.reshape(rows, nb, W), im.reshape(rows, nb, W)], axis=2)
    second = jnp.stack([-im.reshape(rows, nb, W), re.reshape(rows, nb, W)], axis=2)
    return jnp.stack([first, second], axis=1).reshape(2 * rows, 2 * n)


def pad_rows(x, rows):
    return jnp.pad(x, ((0, rows - x.shape[0]), (0, 0)))


def halves(x):
    hi = x.astype(BF16)
    return hi, (x - hi.astype(F32)).astype(BF16)


def rounded_halves(x):
    hi = lax.reduce_precision(x, exponent_bits=8, mantissa_bits=7)
    return hi.astype(BF16), (x - hi).astype(BF16)


def state_exponents(length):
    nb = length // W
    m = np.arange(length)
    rows, masks = [], []
    for b in range(nb):
        rows += [b * W - 1 - m, m - (b + 1) * W]
        masks += [m < b * W, m >= (b + 1) * W]
    rows += [length - 1 - m, m]
    masks += [m >= 0, m >= 0]
    return np.maximum(np.stack(rows), 0).astype(np.int32), np.stack(masks)


def state_matrix(modulus, angle, length):
    exps, masks = state_exponents(length)
    re, im = root_powers(modulus, angle, jnp.asarray(exps))
    masks = jnp.asarray(masks)
    return real_rows((jnp.where(masks, re, 0.0), jnp.where(masks, im, 0.0)))


def link_coefs(modulus, angle, off, end, count, mine, length):
    other = jnp.arange(count, dtype=jnp.int32)
    far = root_powers(modulus, angle, length * (2 * count - 2 - mine - other))
    near = root_powers(modulus, angle, length * jnp.maximum(jnp.abs(other - mine) - 1, 0))
    root = (modulus * jnp.cos(angle), modulus * jnp.sin(angle))
    tail = complex_mul(end, far)
    head = complex_mul(complex_mul(off, root), near)
    before = other < mine
    one = jnp.ones((count,), F32)
    zero = jnp.zeros((count,), F32)
    send_f = (jnp.where(before, tail[0], one), jnp.where(before, tail[1], zero))
    send_b = (jnp.where(before, head[0], zero), jnp.where(before, head[1], zero))
    recv_f = (jnp.where(before, near[0], zero), jnp.where(before, near[1], zero))
    after = other > mine
    recv_b = (jnp.where(after, one, tail[0]), jnp.where(after, zero, tail[1]))
    return jnp.stack([*send_f, *send_b, *recv_f, *recv_b], axis=1)


def split3(x, first):
    hi, lo = halves(x)
    return jnp.concatenate([hi, lo, hi] if first else [hi, hi, lo], axis=0)


def nt(a, b):
    return lax.dot_general(a, b, (((1,), (1,)), ((), ())), preferred_element_type=F32)


def tn(a, b):
    return lax.dot_general(a, b, (((0,), (0,)), ((), ())), preferred_element_type=F32)


def nn(a, b):
    return lax.dot_general(a, b, (((1,), (0,)), ((), ())), preferred_element_type=F32)


def lookup(table, index):
    chunks = table.shape[0]
    out = None
    for c in range(chunks):
        row = jnp.broadcast_to(table[c : c + 1, :], index.shape)
        here = jnp.clip(index - c * W, 0, W - 1) if chunks > 1 else index
        got = jnp.take_along_axis(row, here, axis=1, mode="promise_in_bounds")
        out = got if out is None else jnp.where(index >= c * W, got, out)
    return out


def weigh(coef, row, col, pair):
    cr, ci = coef[row, col], coef[row, col + 1]
    return (cr * pair[0] - ci * pair[1], cr * pair[1] + ci * pair[0])


def add_pair(a, b):
    return b if a is None else (a[0] + b[0], a[1] + b[1])


def gather_entries(coef, recv, count, chain):
    first = second = None
    for e in range(count):
        pair = (recv[e, 2 * chain : 2 * chain + 1, :], recv[e, 2 * chain + 1 : 2 * chain + 2, :])
        first = add_pair(first, weigh(coef, e, 4, pair))
        second = add_pair(second, weigh(coef, e, 6, pair))
    return first, second


def write_pieces(coef, pieces, count, chain, f_pair, b_pair):
    for e in range(count):
        out = add_pair(weigh(coef, e, 0, f_pair), weigh(coef, e, 2, b_pair))
        pieces[e, 2 * chain : 2 * chain + 1, :] = out[0]
        pieces[e, 2 * chain + 1 : 2 * chain + 2, :] = out[1]


def put_turned(t_hi, t_lo, chain, b, pair):
    for part in range(2):
        hi, lo = halves(pair[part])
        t_hi[chain, 0, b * W : (b + 1) * W, part * W : (part + 1) * W] = hi
        t_lo[chain, 0, b * W : (b + 1) * W, part * W : (part + 1) * W] = lo


def y_states(t_hi, t_lo, st3, st_hi, coef_y, y_state, y_pieces, nby, county):
    rows = st_hi.shape[0]
    for chain in range(2):
        acc = jnp.zeros((2 * rows, W), F32)
        low = jnp.zeros((rows, W), F32)
        for b in range(nby):
            lanes = slice(2 * W * b, 2 * W * (b + 1))
            acc = acc + nt(st3[:, lanes], t_hi[chain, 0, b * W : (b + 1) * W, :])
            low = low + nt(st_hi[:, lanes], t_lo[chain, 0, b * W : (b + 1) * W, :])
        total = acc[:rows] + acc[rows:] + low
        y_state[chain] = total
        d = 4 * nby
        write_pieces(
            coef_y, y_pieces, county, chain,
            (total[d : d + 1], total[d + 1 : d + 2]), (total[d + 2 : d + 3], total[d + 3 : d + 4]),
        )


def first_kernel(nby, county, src, rec, idx, table, st3, st_hi, coef_y, t_hi, t_lo, y_state, y_pieces):
    for b in range(nby):
        lanes = slice(b * W, (b + 1) * W)
        put_turned(t_hi, t_lo, 0, b, (src[0, 0, :, lanes], src[1, 0, :, lanes]))
        index = idx[0, :, lanes]
        cos, sin = lookup(table[0], index), lookup(table[1], index)
        put_turned(t_hi, t_lo, 1, b, complex_mul((rec[0, 0, :, lanes], -rec[1, 0, :, lanes]), (cos, sin)))
    y_states(t_hi, t_lo, st3, st_hi, coef_y, y_state, y_pieces, nby, county)


def local_kernel(nby, t_hi, t_lo, y_state, my_hi, my_lo, sp_y, lx_h, lx_l, w_out, x_state, vx_hi, vx_lo):
    a = pl.program_id(1)
    srows = lx_l.shape[1] - 2 * W
    main = nn(t_hi[0, 0], my_hi[...]) + nn(t_hi[0, 0], my_lo[...]) + nn(t_lo[0, 0], my_hi[...])
    for b in range(nby):
        st = split3(y_state[0, 4 * b : 4 * b + 4, :], True)
        v = main[b * W : (b + 1) * W] + tn(st, sp_y[...])
        hi, lo = halves(v)
        for part in range(2):
            vx_hi[part * W : (part + 1) * W, b * W : (b + 1) * W] = hi[:, part * W : (part + 1) * W]
            vx_lo[part * W : (part + 1) * W, b * W : (b + 1) * W] = lo[:, part * W : (part + 1) * W]
    high = nn(lx_h[0], vx_hi[...])
    low = nn(lx_l[0], vx_lo[...])
    w_out[0, 0] = high[: 2 * W] + high[2 * W : 4 * W] + low[: 2 * W]
    states = high[4 * W : 4 * W + srows] + high[4 * W + srows :] + low[2 * W :]

    @pl.when(a == 0)
    def _():
        x_state[0] = states

    @pl.when(a > 0)
    def _():
        x_state[0] += states


def link_kernel(
    nbx, county, countx, recv_y, x_local, coef_y, coef_x, sx, edge, mxt, x_state, ym, x_pieces
):
    for chain in range(2):
        (fr, fi), (br, bi) = gather_entries(coef_y, recv_y, county, chain)
        cols = []
        for a in range(nbx):
            lanes = slice(a * W, (a + 1) * W)
            top = jnp.concatenate([fr[:, lanes], fi[:, lanes]], axis=1)
            top2 = jnp.concatenate([-fi[:, lanes], fr[:, lanes]], axis=1)
            bot = jnp.concatenate([br[:, lanes], bi[:, lanes]], axis=1)
            bot2 = jnp.concatenate([-bi[:, lanes], br[:, lanes]], axis=1)
            cols.append(jnp.concatenate([top, top2, bot, bot2, jnp.zeros((4, 2 * W), F32)], axis=0))
        gain = None
        for a in range(nbx):
            ym[chain, :, 2 * W * a : 2 * W * (a + 1)] = lax.dot_general(
                cols[a], mxt[...], (((1,), (0,)), ((), ())), precision=HIGHEST, preferred_element_type=F32
            )
            part = lax.dot_general(
                sx[:, 2 * W * a : 2 * W * (a + 1)], cols[a], (((1,), (1,)), ((), ())),
                precision=HIGHEST, preferred_element_type=F32,
            )
            gain = part if gain is None else gain + part
        total = x_local[chain]
        for s in range(4):
            total = total + gain[:, s : s + 1] * edge[s : s + 1, :]
        for a in range(nbx):
            x_state[chain, a, 0:4, :] = total[4 * a : 4 * a + 4, :]
            x_state[chain, a, 4:8, :] = jnp.zeros((4, total.shape[1]), F32)
        d = 4 * nbx
        write_pieces(
            coef_x, x_pieces, countx, chain,
            (total[d : d + 1], total[d + 1 : d + 2]), (total[d + 2 : d + 3], total[d + 3 : d + 4]),
        )


def post_kernel(plan, nby, county, countx, *refs):
    refs = list(refs)
    take = lambda: refs.pop(0)
    w_in, x_state, ym, recv_x, coef_x, edge, sp_x, sp_dev, table = (take() for _ in range(9))
    idx_s = take()
    idx_r = take() if plan["turn"] else None
    st3, st_hi, coef_y = (take(), take(), take()) if plan["turn"] else (None,) * 3
    olds = [{"s": (take(), take()) if z[1] == "split" else take() if z[1] == "field" else None,
             "r": take() if z[2] else None} for z in plan["images"]]
    if plan["turn"]:
        t_hi, t_lo, y_state, y_pieces = (take() for _ in range(4))
    else:
        src_out, rec_out = take(), take()
    keep_out = take() if plan["keep"] else None
    image_outs = [take() for _ in plan["images"]]

    lefts, rights = [], []
    for chain in range(2):
        first, second = gather_entries(coef_x, recv_x, countx, chain)
        mine = x_state[chain, 0, 0:4, :]
        right = jnp.concatenate([mine, *first, *second, edge[0:4, :]], axis=0)
        left = jnp.concatenate([sp_x[...], sp_dev[0], ym[chain, 0:4, :]], axis=0)
        rights.append(split3(right, False))
        lefts.append(split3(left, True))
    for b in range(nby):
        lanes = slice(b * W, (b + 1) * W)
        fields = []
        for chain in range(2):
            u = w_in[chain, 0, :, lanes] + tn(lefts[chain], rights[chain][:, lanes])
            fields.append((u[:W], u[W:]))
        index = idx_s[0, :, lanes]
        source = complex_mul(fields[0], (lookup(table[0], index), lookup(table[1], index)))
        back = fields[1]
        if plan["turn"]:
            put_turned(t_hi, t_lo, 0, b, source)
            index = idx_r[0, :, lanes]
            put_turned(t_hi, t_lo, 1, b, complex_mul(back, (lookup(table[0], index), lookup(table[1], index))))
        else:
            src_out[0, 0, :, lanes], src_out[1, 0, :, lanes] = source
            rec_out[0, 0, :, lanes], rec_out[1, 0, :, lanes] = back[0], -back[1]
        if keep_out is not None:
            keep_out[0, :, lanes], keep_out[1, :, lanes] = back
        for old, (_, how, has_r), out in zip(olds, plan["images"], image_outs):
            if how == "split":
                hi, lo = old["s"]
                rows = slice(b * W, (b + 1) * W)
                s = [hi[0, 0, rows, p * W : (p + 1) * W].astype(F32) + lo[0, 0, rows, p * W : (p + 1) * W].astype(F32)
                     for p in range(2)]
            elif how == "field":
                s = (old["s"][0, 0, :, lanes], old["s"][1, 0, :, lanes])
            else:
                s = source
            r = (old["r"][0, :, lanes], old["r"][1, :, lanes]) if has_r else back
            out[:, lanes] = s[0] * r[0] - s[1] * r[1]
    if plan["turn"]:
        y_states(t_hi, t_lo, st3, st_hi, coef_y, y_state, y_pieces, nby, county)


def whole(shape):
    return pl.BlockSpec(shape, lambda *_: (0,) * len(shape))


SMEM = pl.BlockSpec(memory_space=pltpu.SMEM)


def params(dims):
    return pltpu.CompilerParams(vmem_limit_bytes=VMEM_LIMIT, dimension_semantics=("arbitrary",) * dims)


def on_device(source_field, receiver_field, velocity_index, slowness, freq_index, root_modulus, root_angle):
    depth, len_x, len_y = velocity_index.shape
    nbx, nby = len_x // W, len_y // W
    countx, county = lax.axis_size("gx"), lax.axis_size("gy")
    modulus, angle = root_modulus[0], root_angle[0]
    diag, off, end = sweep_factors(modulus, angle)

    entries = slowness.shape[0]
    chunks = -(-entries // W)
    rate = freq_index.astype(F32)[0] * PHASE_UNIT
    phase = jnp.pad(rate * slowness, (0, chunks * W - entries)).reshape(chunks, W)
    table = jnp.stack([jnp.cos(phase), jnp.sin(phase)])

    at = np.arange(W)
    dist = np.abs(at[:, None] - at[None, :]).astype(np.int32)
    pw = root_powers(modulus, angle, jnp.asarray(dist))
    pw = complex_mul(off, pw)
    on = jnp.asarray(dist == 0)
    mr, mi = jnp.where(on, diag[0], pw[0]), jnp.where(on, diag[1], pw[1])
    my = jnp.concatenate([jnp.concatenate([mr, mi], 1), jnp.concatenate([-mi, mr], 1)], 0)
    mx = jnp.concatenate([jnp.concatenate([mr, -mi], 1), jnp.concatenate([mi, mr], 1)], 0)
    my_hi, my_lo = rounded_halves(my)
    mx_hi, mx_lo = rounded_halves(mx)

    rows_y = -(-(4 * nby + 4) // 16) * 16
    rows_x = -(-(4 * nbx + 4) // 16) * 16
    st_hi, st_lo = rounded_halves(pad_rows(state_matrix(modulus, angle, len_y), rows_y))
    st3 = jnp.concatenate([st_hi, st_lo], axis=0)
    sx = pad_rows(state_matrix(modulus, angle, len_x), rows_x)
    sx_hi, sx_lo = rounded_halves(sx)
    blocks_of = lambda x: x.reshape(rows_x, nbx, 2 * W).transpose(1, 0, 2)
    rep = lambda x: jnp.broadcast_to(x[None], (nbx,) + x.shape)
    lx_h = jnp.concatenate([rep(mx_hi), rep(mx_lo), blocks_of(sx_hi), blocks_of(sx_lo)], axis=1)
    lx_l = jnp.concatenate([rep(mx_hi), blocks_of(sx_hi)], axis=1)

    near = complex_mul(off, root_powers(modulus, angle, jnp.asarray(np.stack([at + 1, W - at]).astype(np.int32))))
    spread = spread_rows(near)
    sp_hi, sp_lo = rounded_halves(spread)
    sp_y = jnp.concatenate([sp_hi, sp_hi, sp_lo], axis=0)

    def edges(length):
        m = np.arange(length)
        ahead = complex_mul(off, root_powers(modulus, angle, jnp.asarray((m + 1).astype(np.int32))))
        behind = root_powers(modulus, angle, jnp.asarray((length - 1 - m).astype(np.int32)))
        return jnp.stack([ahead[0], behind[0]]), jnp.stack([ahead[1], behind[1]])

    edge_x = spread_rows(edges(len_x)).reshape(4, nbx, 2 * W).transpose(1, 0, 2)
    er, ei = edges(len_y)
    edge_y = jnp.concatenate([jnp.stack([er, ei], axis=1).reshape(4, len_y), jnp.zeros((4, len_y), F32)], axis=0)

    coef_y = link_coefs(modulus, angle, off, end, county, lax.axis_index("gy"), len_y)
    coef_x = link_coefs(modulus, angle, off, end, countx, lax.axis_index("gx"), len_x)

    turned = jax.ShapeDtypeStruct((2, nbx, nby * W, 2 * W), BF16)
    turned_spec = pl.BlockSpec((2, 1, nby * W, 2 * W), lambda a: (0, a, 0, 0))
    y_state_shape = jax.ShapeDtypeStruct((2, rows_y, len_x), F32)
    y_state_spec = pl.BlockSpec((2, rows_y, W), lambda a: (0, 0, a))
    y_piece_shape = jax.ShapeDtypeStruct((county, 4, len_x), F32)
    y_piece_spec = pl.BlockSpec((county, 4, W), lambda a: (0, 0, a))
    field_spec = pl.BlockSpec((2, 1, W, len_y), lambda a: (0, 0, a, 0))
    keep_spec = pl.BlockSpec((2, W, len_y), lambda a: (0, a, 0))
    image_spec = pl.BlockSpec((W, len_y), lambda a: (a, 0))
    level_spec = lambda z: pl.BlockSpec((1, W, len_y), lambda a: (z, a, 0))
    turn_out = [turned, turned, y_state_shape, y_piece_shape]
    turn_specs = [turned_spec, turned_spec, y_state_spec, y_piece_spec]

    t_hi, t_lo, y_state, y_pieces = pl.pallas_call(
        functools.partial(first_kernel, nby, county),
        grid=(nbx,),
        in_specs=[field_spec, field_spec, level_spec(depth - 1), whole(table.shape), whole(st3.shape),
                  whole(st_hi.shape), SMEM],
        out_specs=turn_specs,
        out_shape=turn_out,
        compiler_params=params(1),
        name="first",
    )(source_field, receiver_field, velocity_index, table, st3, st_hi, coef_y)

    local = pl.pallas_call(
        functools.partial(local_kernel, nby),
        grid=(2, nbx),
        in_specs=[
            pl.BlockSpec((1, 1, nby * W, 2 * W), lambda c, a: (c, a, 0, 0)),
            pl.BlockSpec((1, 1, nby * W, 2 * W), lambda c, a: (c, a, 0, 0)),
            pl.BlockSpec((1, rows_y, W), lambda c, a: (c, 0, a)),
            whole(my_hi.shape), whole(my_lo.shape), whole(sp_y.shape),
            pl.BlockSpec((1,) + lx_h.shape[1:], lambda c, a: (a, 0, 0)),
            pl.BlockSpec((1,) + lx_l.shape[1:], lambda c, a: (a, 0, 0)),
        ],
        out_specs=[
            pl.BlockSpec((1, 1, 2 * W, len_y), lambda c, a: (c, a, 0, 0)),
            pl.BlockSpec((1, rows_x, len_y), lambda c, a: (c, 0, 0)),
        ],
        out_shape=[
            jax.ShapeDtypeStruct((2, nbx, 2 * W, len_y), F32),
            jax.ShapeDtypeStruct((2, rows_x, len_y), F32),
        ],
        scratch_shapes=[pltpu.VMEM((2 * W, len_y), BF16)] * 2,
        compiler_params=params(2),
        name="local",
    )

    link = pl.pallas_call(
        functools.partial(link_kernel, nbx, county, countx),
        in_specs=[pl.BlockSpec(memory_space=pltpu.VMEM)] * 2 + [SMEM] * 2 + [pl.BlockSpec(memory_space=pltpu.VMEM)] * 3,
        out_shape=[
            jax.ShapeDtypeStruct((2, nbx, 8, len_y), F32),
            jax.ShapeDtypeStruct((2, 8, 2 * len_x), F32),
            jax.ShapeDtypeStruct((countx, 4, len_y), F32),
        ],
        compiler_params=params(0),
        name="link",
    )

    source_levels = {0: ("field", (source_field,))}
    kept = {}
    images = [None] * depth
    for step in range(depth):
        w, x_local = local(t_hi, t_lo, y_state, my_hi, my_lo, sp_y, lx_h, lx_l)
        recv_y = lax.all_to_all(y_pieces, "gy", 0, 0)
        x_state, ym, x_pieces = link(recv_y, x_local, coef_y, coef_x, sx, edge_y, mx.T)
        recv_x = lax.all_to_all(x_pieces, "gx", 0, 0)
        turn = step < depth - 1
        level_r = depth - 1 - step
        todo = [z for z in range(depth) if max(z - 1, depth - 1 - z) == step]
        plan = {
            "turn": turn,
            "keep": level_r - 1 > step,
            "images": [(z, None if z - 1 == step else source_levels[z][0], z != level_r) for z in todo],
        }
        args = [w, x_state, ym, recv_x, coef_x, edge_y, spread, edge_x, table, velocity_index]
        specs = [
            pl.BlockSpec((2, 1, 2 * W, len_y), lambda a: (0, a, 0, 0)),
            pl.BlockSpec((2, 1, 8, len_y), lambda a: (0, a, 0, 0)),
            pl.BlockSpec((2, 8, 2 * W), lambda a: (0, 0, a)),
            whole(recv_x.shape), SMEM, whole(edge_y.shape), whole(spread.shape),
            pl.BlockSpec((1, 4, 2 * W), lambda a: (a, 0, 0)),
            whole(table.shape), level_spec(step),
        ]
        if turn:
            args += [velocity_index, st3, st_hi, coef_y]
            specs += [level_spec(depth - 2 - step), whole(st3.shape), whole(st_hi.shape), SMEM]
        for z, how, has_r in plan["images"]:
            if how == "split":
                args += source_levels[z][1]
                specs += [pl.BlockSpec((1, 1, nby * W, 2 * W), lambda a: (0, a, 0, 0))] * 2
            elif how == "field":
                args += source_levels[z][1]
                specs += [field_spec]
            if has_r:
                args += [kept[z]]
                specs += [keep_spec]
        if turn:
            shapes, out_specs = list(turn_out), list(turn_specs)
        else:
            shapes = [jax.ShapeDtypeStruct(source_field.shape, F32)] * 2
            out_specs = [field_spec] * 2
        if plan["keep"]:
            shapes.append(jax.ShapeDtypeStruct((2, len_x, len_y), F32))
            out_specs.append(keep_spec)
        shapes += [jax.ShapeDtypeStruct((len_x, len_y), F32)] * len(todo)
        out_specs += [image_spec] * len(todo)
        outs = pl.pallas_call(
            functools.partial(post_kernel, plan, nby, county, countx),
            grid=(nbx,),
            in_specs=specs,
            out_specs=out_specs,
            out_shape=shapes,
            compiler_params=params(1),
            name="post",
        )(*args)
        outs = list(outs)
        if turn:
            t_hi, t_lo, y_state, y_pieces = outs[:4]
            outs = outs[4:]
            source_levels[step + 1] = ("split", (t_hi, t_lo))
        else:
            source, receiver = outs[:2]
            outs = outs[2:]
        if plan["keep"]:
            kept[level_r] = outs.pop(0)
        for z in todo:
            images[z] = outs.pop(0)
    return jnp.stack(images), source, receiver


def solution(mesh):
    placed = (
        P(None, None, "gx", "gy"),
        P(None, None, "gx", "gy"),
        P(None, "gx", "gy"),
        P(),
        P(),
        P(),
        P(),
    )
    return jax.shard_map(
        on_device,
        mesh=mesh,
        in_specs=placed,
        out_specs=(P(None, "gx", "gy"), P(None, None, "gx", "gy"), P(None, None, "gx", "gy")),
        check_vma=False,
    )
```

```python
import functools

import jax
import jax.numpy as jnp
import numpy as np
from jax import lax
from jax.experimental import pallas as pl
from jax.experimental.pallas import tpu as pltpu
from jax.sharding import PartitionSpec as P

PHASE_UNIT = 0.05
W = 128
F32 = jnp.float32
BF16 = jnp.bfloat16
HIGHEST = lax.Precision.HIGHEST
MIB = 1024 * 1024


def complex_mul(a, b):
    return (a[0] * b[0] - a[1] * b[1], a[0] * b[1] + a[1] * b[0])


def root_powers(modulus, angle, exponent):
    k = exponent.astype(F32)
    coarse = jnp.round(angle * 512.0)
    fine = angle - coarse * (1.0 / 512.0)
    steps = k * coarse
    turns = jnp.round(steps * np.float32(1.0 / 512.0 / (2.0 * np.pi)))
    spin = (steps * (1.0 / 512.0) - turns * 6.28125) - turns * np.float32(2.0 * np.pi - 6.28125)
    spin = spin + k * fine
    magnitude = jnp.exp(jnp.log(modulus) * k)
    return (magnitude * jnp.cos(spin), magnitude * jnp.sin(spin))


def sweep_factors(modulus, angle):
    sin, cos = jnp.sin(angle), jnp.cos(angle)
    gap = (1.0 - modulus) * (1.0 + modulus)
    re, im = modulus * cos, modulus * sin
    den_re, den_im = gap + 2.0 * im * im, -2.0 * re * im
    den_sq = den_re * den_re + den_im * den_im
    inv = (den_re / den_sq, -den_im / den_sq)
    diag = (re * re - im * im + gap * gap * inv[0], -2.0 * re * im + gap * gap * inv[1])
    root_inv = (re / (modulus * modulus), -im / (modulus * modulus))
    off = complex_mul((0.0 * im, 2.0 * gap * im), complex_mul(root_inv, inv))
    end = (-gap * gap * inv[0], -gap * gap * inv[1])
    return diag, off, end


def real_rows(pair):
    re, im = pair
    rows, n = re.shape
    nb = n // W
    first = jnp.stack([re.reshape(rows, nb, W), -im.reshape(rows, nb, W)], axis=2)
    second = jnp.stack([im.reshape(rows, nb, W), re.reshape(rows, nb, W)], axis=2)
    return jnp.stack([first, second], axis=1).reshape(2 * rows, 2 * n)


def spread_rows(pair):
    re, im = pair
    rows, n = re.shape
    nb = n // W
    first = jnp.stack([re.reshape(rows, nb, W), im.reshape(rows, nb, W)], axis=2)
    second = jnp.stack([-im.reshape(rows, nb, W), re.reshape(rows, nb, W)], axis=2)
    return jnp.stack([first, second], axis=1).reshape(2 * rows, 2 * n)


def pad_rows(x, rows):
    return jnp.pad(x, ((0, rows - x.shape[0]), (0, 0)))


def halves(x):
    hi = x.astype(BF16)
    return hi, (x - hi.astype(F32)).astype(BF16)


def rounded_halves(x):
    hi = lax.reduce_precision(x, exponent_bits=8, mantissa_bits=7)
    return hi.astype(BF16), (x - hi).astype(BF16)


def state_exponents(length):
    nb = length // W
    m = np.arange(length)
    rows, masks = [], []
    for b in range(nb):
        rows += [b * W - 1 - m, m - (b + 1) * W]
        masks += [m < b * W, m >= (b + 1) * W]
    rows += [length - 1 - m, m]
    masks += [m >= 0, m >= 0]
    return np.maximum(np.stack(rows), 0).astype(np.int32), np.stack(masks)


def state_matrix(modulus, angle, length):
    exps, masks = state_exponents(length)
    re, im = root_powers(modulus, angle, jnp.asarray(exps))
    masks = jnp.asarray(masks)
    return real_rows((jnp.where(masks, re, 0.0), jnp.where(masks, im, 0.0)))


def partner(mine, slot, count, way):
    if count & (count - 1) == 0:
        return mine ^ slot
    return (mine + way * slot) % count


def exchange(pieces, axis):
    count = len(pieces)
    got = [pieces[0]]
    for s in range(1, count):
        pairs = [(d, partner(d, s, count, 1)) for d in range(count)]
        got.append(lax.ppermute(pieces[s], axis, pairs))
    return got


def link_coefs(modulus, angle, off, end, count, mine, length):
    slots = np.arange(count, dtype=np.int32)
    root = (modulus * jnp.cos(angle), modulus * jnp.sin(angle))
    one = jnp.ones((count,), F32)
    zero = jnp.zeros((count,), F32)

    def factors(other):
        far = root_powers(modulus, angle, length * (2 * count - 2 - mine - other))
        near = root_powers(modulus, angle, length * jnp.maximum(jnp.abs(other - mine) - 1, 0))
        return near, complex_mul(end, far)

    other = partner(mine, slots, count, 1)
    near, tail = factors(other)
    head = complex_mul(complex_mul(off, root), near)
    before = other < mine
    send_f = (jnp.where(before, tail[0], one), jnp.where(before, tail[1], zero))
    send_b = (jnp.where(before, head[0], zero), jnp.where(before, head[1], zero))
    other = partner(mine, slots, count, -1)
    near, tail = factors(other)
    before, after = other < mine, other > mine
    recv_f = (jnp.where(before, near[0], zero), jnp.where(before, near[1], zero))
    recv_b = (jnp.where(after, one, tail[0]), jnp.where(after, zero, tail[1]))
    return jnp.stack([*send_f, *send_b, *recv_f, *recv_b], axis=1)


def split3(x, first):
    hi, lo = halves(x)
    return jnp.concatenate([hi, lo, hi] if first else [hi, hi, lo], axis=0)


def nt(a, b):
    return lax.dot_general(a, b, (((1,), (1,)), ((), ())), preferred_element_type=F32)


def tn(a, b):
    return lax.dot_general(a, b, (((0,), (0,)), ((), ())), preferred_element_type=F32)


def nn(a, b):
    return lax.dot_general(a, b, (((1,), (0,)), ((), ())), preferred_element_type=F32)


def lookup(table, index):
    chunks = table.shape[0]
    out = None
    for c in range(chunks):
        row = jnp.broadcast_to(table[c : c + 1, :], index.shape)
        here = jnp.clip(index - c * W, 0, W - 1) if chunks > 1 else index
        got = jnp.take_along_axis(row, here, axis=1, mode="promise_in_bounds")
        out = got if out is None else jnp.where(index >= c * W, got, out)
    return out


def weigh(coef, row, col, pair):
    cr, ci = coef[row, col], coef[row, col + 1]
    return (cr * pair[0] - ci * pair[1], cr * pair[1] + ci * pair[0])


def add_pair(a, b):
    return b if a is None else (a[0] + b[0], a[1] + b[1])


def gather_entries(coef, recv, count, chain):
    first = second = None
    for e in range(count):
        pair = (recv[e][2 * chain : 2 * chain + 1, :], recv[e][2 * chain + 1 : 2 * chain + 2, :])
        first = add_pair(first, weigh(coef, e, 4, pair))
        second = add_pair(second, weigh(coef, e, 6, pair))
    return first, second


def write_pieces(coef, pieces, count, chain, f_pair, b_pair):
    for e in range(count):
        out = add_pair(weigh(coef, e, 0, f_pair), weigh(coef, e, 2, b_pair))
        pieces[e][2 * chain : 2 * chain + 1, :] = out[0]
        pieces[e][2 * chain + 1 : 2 * chain + 2, :] = out[1]


def put_turned(t_hi, t_lo, chain, b, pair):
    for part in range(2):
        hi, lo = halves(pair[part])
        t_hi[chain, 0, b * W : (b + 1) * W, part * W : (part + 1) * W] = hi
        t_lo[chain, 0, b * W : (b + 1) * W, part * W : (part + 1) * W] = lo


def add_states(acc, t_hi, t_lo, st, b):
    rows = slice(b * W, (b + 1) * W)
    high = jnp.concatenate([t_hi[0, 0, rows, :], t_hi[1, 0, rows, :]], axis=0)
    low = jnp.concatenate([t_lo[0, 0, rows, :], t_lo[1, 0, rows, :]], axis=0)
    part = nn(jnp.concatenate([high, low], axis=1), st[b])
    return part if acc is None else acc + part


def put_states(acc, coef_y, y_state, y_pieces, nby, county):
    half = acc.shape[1] // 2
    rows = y_state.shape[2]
    turned = acc.T
    both = turned[:rows] + turned[half : half + rows]
    d = 4 * nby
    for chain in range(2):
        total = both[:, chain * W : (chain + 1) * W]
        y_state[chain, 0] = total
        write_pieces(
            coef_y, y_pieces, county, chain,
            (total[d : d + 1], total[d + 1 : d + 2]), (total[d + 2 : d + 3], total[d + 3 : d + 4]),
        )


def first_kernel(nby, county, src, rec, idx, table, st, coef_y, early, t_hi, t_lo, y_state, *y_pieces):
    acc = None
    for b in range(nby):
        lanes = slice(b * W, (b + 1) * W)
        put_turned(t_hi, t_lo, 0, b, (src[0, 0, :, lanes], src[1, 0, :, lanes]))
        index = idx[0, :, lanes]
        cos, sin = lookup(table[0], index), lookup(table[1], index)
        put_turned(t_hi, t_lo, 1, b, complex_mul((rec[0, 0, :, lanes], -rec[1, 0, :, lanes]), (cos, sin)))
        acc = add_states(acc, t_hi, t_lo, st, b)
    put_states(acc, coef_y, y_state, y_pieces, nby, county)


def local_kernel(nbx, nby, t_hi, t_lo, y_state, my3, sp_y, lx, w_out, x_state, vx_hi, vx_lo):
    x_state[...] = jnp.zeros_like(x_state)

    def block(i, carry):
        c, a = i // nbx, i % nbx
        state = y_state[c, a]
        for j in range(0, nby, 2):
            rows = slice(j * W, (j + 2) * W)
            high, low = t_hi[c, a, rows, :], t_lo[c, a, rows, :]
            main = nn(jnp.concatenate([high, low, high], axis=1), my3[...])
            for b in (j, j + 1):
                v = main[(b - j) * W : (b - j + 1) * W] + tn(split3(state[4 * b : 4 * b + 4, :], True), sp_y[...])
                hi, lo = halves(v)
                for part in range(2):
                    at = slice(part * W, (part + 1) * W)
                    vx_hi[at, b * W : (b + 1) * W] = hi[:, at]
                    vx_lo[at, b * W : (b + 1) * W] = lo[:, at]
        left = lx[a]
        for j in range(0, nby, 2):
            lanes = slice(j * W, (j + 2) * W)
            high, low = vx_hi[:, lanes], vx_lo[:, lanes]
            out = nn(left, jnp.concatenate([high, low, high], axis=0))
            w_out[c, a, :, lanes] = out[: 2 * W]
            x_state[c, :, lanes] += out[2 * W :]
        return carry

    lax.fori_loop(0, 2 * nbx, block, 0)


def link_kernel(
    nbx, county, countx, x_local, coef_y, coef_x, sx, edge, mxt, *refs
):
    recv_y, (x_state, ym), x_pieces = refs[:county], refs[county : county + 2], refs[county + 2 :]
    for chain in range(2):
        (fr, fi), (br, bi) = gather_entries(coef_y, recv_y, county, chain)
        cols = []
        for a in range(nbx):
            lanes = slice(a * W, (a + 1) * W)
            top = jnp.concatenate([fr[:, lanes], fi[:, lanes]], axis=1)
            top2 = jnp.concatenate([-fi[:, lanes], fr[:, lanes]], axis=1)
            bot = jnp.concatenate([br[:, lanes], bi[:, lanes]], axis=1)
            bot2 = jnp.concatenate([-bi[:, lanes], br[:, lanes]], axis=1)
            cols.append(jnp.concatenate([top, top2, bot, bot2, jnp.zeros((4, 2 * W), F32)], axis=0))
        gain = None
        for a in range(nbx):
            ym[chain, :, 2 * W * a : 2 * W * (a + 1)] = lax.dot_general(
                cols[a], mxt[...], (((1,), (0,)), ((), ())), precision=HIGHEST, preferred_element_type=F32
            )
            part = lax.dot_general(
                sx[:, 2 * W * a : 2 * W * (a + 1)], cols[a], (((1,), (1,)), ((), ())),
                precision=HIGHEST, preferred_element_type=F32,
            )
            gain = part if gain is None else gain + part
        total = x_local[chain]
        for s in range(4):
            total = total + gain[:, s : s + 1] * edge[s : s + 1, :]
        for a in range(nbx):
            x_state[chain, a, 0:4, :] = total[4 * a : 4 * a + 4, :]
            x_state[chain, a, 4:8, :] = jnp.zeros((4, total.shape[1]), F32)
        d = 4 * nbx
        write_pieces(
            coef_x, x_pieces, countx, chain,
            (total[d : d + 1], total[d + 1 : d + 2]), (total[d + 2 : d + 3], total[d + 3 : d + 4]),
        )


def post_kernel(plan, nby, county, countx, *refs):
    refs = list(refs)
    take = lambda: refs.pop(0)
    w_in, x_state, ym, coef_x, edge, sp_x, sp_dev, table = (take() for _ in range(8))
    recv_x = [take() for _ in range(countx)]
    idx_s = take()
    idx_r = take() if plan["turn"] else None
    st, coef_y = (take(), take()) if plan["turn"] else (None, None)
    olds = [{"s": (take(), take()) if z[1] == "split" else take() if z[1] == "field" else None,
             "r": take() if z[2] else None} for z in plan["images"]]
    if plan["alias"]:
        take()
    if plan["turn"]:
        t_hi, t_lo, y_state = (take() for _ in range(3))
        y_pieces = [take() for _ in range(county)]
    else:
        src_out, rec_out = take(), take()
    keep_out = take() if plan["keep"] else None
    image = take() if plan["images"] else None
    if plan["images"]:
        slots, sems = take(), take()
    a, last = pl.program_id(0), pl.num_programs(0) - 1
    slot = lax.rem(a, 2)

    def image_copy(n, at, slot):
        rows = pl.ds(pl.multiple_of(at * W, W), W)
        return pltpu.make_async_copy(slots.at[n, slot], image.at[plan["images"][n][0], rows], sems.at[n, slot])

    for n in range(len(plan["images"])):
        @pl.when(a >= 2)
        def _():
            image_copy(n, a - 2, slot).wait()

    acc = None
    lefts, rights = [], []
    for chain in range(2):
        first, second = gather_entries(coef_x, recv_x, countx, chain)
        mine = x_state[chain, 0, 0:4, :]
        right = jnp.concatenate([mine, *first, *second, edge[0:4, :]], axis=0)
        left = jnp.concatenate([sp_x[...], sp_dev[0], ym[chain, 0:4, :]], axis=0)
        rights.append(split3(right, False))
        lefts.append(split3(left, True))
    for b in range(nby):
        lanes = slice(b * W, (b + 1) * W)
        if b % 2 == 0:
            wide = slice(b * W, min(b + 2, nby) * W)
            fixes = [tn(lefts[chain], rights[chain][:, wide]) for chain in range(2)]
        fields = []
        for chain in range(2):
            u = w_in[chain, 0, :, lanes] + fixes[chain][:, b % 2 * W : (b % 2 + 1) * W]
            fields.append((u[:W], u[W:]))
        index = idx_s[0, :, lanes]
        source = complex_mul(fields[0], (lookup(table[0], index), lookup(table[1], index)))
        back = fields[1]
        if plan["turn"]:
            put_turned(t_hi, t_lo, 0, b, source)
            index = idx_r[0, :, lanes]
            put_turned(t_hi, t_lo, 1, b, complex_mul(back, (lookup(table[0], index), lookup(table[1], index))))
            acc = add_states(acc, t_hi, t_lo, st, b)
        else:
            src_out[0, 0, :, lanes], src_out[1, 0, :, lanes] = source
            rec_out[0, 0, :, lanes], rec_out[1, 0, :, lanes] = back[0], -back[1]
        if keep_out is not None:
            keep_out[0, :, lanes], keep_out[1, :, lanes] = back
        for n, (old, (_, how, has_r)) in enumerate(zip(olds, plan["images"])):
            if how == "split":
                hi, lo = old["s"]
                rows = slice(b * W, (b + 1) * W)
                s = [hi[0, 0, rows, p * W : (p + 1) * W].astype(F32) + lo[0, 0, rows, p * W : (p + 1) * W].astype(F32)
                     for p in range(2)]
            elif how == "field":
                s = (old["s"][0, 0, :, lanes], old["s"][1, 0, :, lanes])
            else:
                s = source
            r = (old["r"][0, :, lanes], old["r"][1, :, lanes]) if has_r else back
            slots[n, slot, :, lanes] = s[0] * r[0] - s[1] * r[1]
    if plan["turn"]:
        put_states(acc, coef_y, y_state, y_pieces, nby, county)
    for n in range(len(plan["images"])):
        image_copy(n, a, slot).start()

        @pl.when((a == last) & (a >= 1))
        def _():
            image_copy(n, a - 1, 1 - slot).wait()

        @pl.when(a == last)
        def _():
            image_copy(n, a, slot).wait()


def whole(shape):
    return pl.BlockSpec(shape, lambda *_: (0,) * len(shape))


SMEM = pl.BlockSpec(memory_space=pltpu.SMEM)
VMEM = pl.BlockSpec(memory_space=pltpu.VMEM)


def in_hbm(x):
    return pltpu.with_memory_space_constraint(x, pltpu.HBM)


def params(mib):
    return pltpu.CompilerParams(vmem_limit_bytes=mib * MIB)


def on_device(source_field, receiver_field, velocity_index, slowness, freq_index, root_modulus, root_angle):
    depth, len_x, len_y = velocity_index.shape
    nbx, nby = len_x // W, len_y // W
    countx, county = lax.axis_size("gx"), lax.axis_size("gy")
    modulus, angle = root_modulus[0], root_angle[0]
    diag, off, end = sweep_factors(modulus, angle)

    entries = slowness.shape[0]
    chunks = -(-entries // W)
    rate = freq_index.astype(F32)[0] * PHASE_UNIT
    phase = jnp.pad(rate * slowness, (0, chunks * W - entries)).reshape(chunks, W)
    table = jnp.stack([jnp.cos(phase), jnp.sin(phase)])

    at = np.arange(W)
    dist = np.abs(at[:, None] - at[None, :]).astype(np.int32)
    pw = root_powers(modulus, angle, jnp.asarray(dist))
    pw = complex_mul(off, pw)
    on = jnp.asarray(dist == 0)
    mr, mi = jnp.where(on, diag[0], pw[0]), jnp.where(on, diag[1], pw[1])
    my = jnp.concatenate([jnp.concatenate([mr, mi], 1), jnp.concatenate([-mi, mr], 1)], 0)
    mx = jnp.concatenate([jnp.concatenate([mr, -mi], 1), jnp.concatenate([mi, mr], 1)], 0)
    my_hi, my_lo = rounded_halves(my)
    mx_hi, mx_lo = rounded_halves(mx)

    rows_y = -(-(4 * nby + 4) // 16) * 16
    rows_x = -(-(4 * nbx + 4) // 16) * 16
    st_hi, st_lo = rounded_halves(pad_rows(state_matrix(modulus, angle, len_y), -(-rows_y // 64) * 64))
    st = jnp.concatenate([jnp.concatenate([st_hi, st_lo], axis=0), jnp.concatenate([st_hi, 0 * st_lo], axis=0)], axis=1)
    st = st.reshape(st.shape[0], 2, nby, 2 * W).transpose(2, 1, 3, 0).reshape(nby, 4 * W, st.shape[0])
    sx = pad_rows(state_matrix(modulus, angle, len_x), rows_x)
    sx_hi, sx_lo = rounded_halves(sx)
    lx = jnp.concatenate([
        jnp.broadcast_to(jnp.concatenate([mx_hi, mx_hi, mx_lo], axis=1)[None], (nbx, 2 * W, 6 * W)),
        jnp.concatenate([x.reshape(rows_x, nbx, 2 * W).transpose(1, 0, 2) for x in (sx_hi, sx_hi, sx_lo)], axis=2),
    ], axis=1)
    my3 = jnp.concatenate([my_hi, my_hi, my_lo], axis=0)

    near = complex_mul(off, root_powers(modulus, angle, jnp.asarray(np.stack([at + 1, W - at]).astype(np.int32))))
    spread = spread_rows(near)
    sp_hi, sp_lo = rounded_halves(spread)
    sp_y = jnp.concatenate([sp_hi, sp_hi, sp_lo], axis=0)

    def edges(length):
        m = np.arange(length)
        ahead = complex_mul(off, root_powers(modulus, angle, jnp.asarray((m + 1).astype(np.int32))))
        behind = root_powers(modulus, angle, jnp.asarray((length - 1 - m).astype(np.int32)))
        return jnp.stack([ahead[0], behind[0]]), jnp.stack([ahead[1], behind[1]])

    edge_x = spread_rows(edges(len_x)).reshape(4, nbx, 2 * W).transpose(1, 0, 2)
    er, ei = edges(len_y)
    edge_y = jnp.concatenate([jnp.stack([er, ei], axis=1).reshape(4, len_y), jnp.zeros((4, len_y), F32)], axis=0)

    coef_y = link_coefs(modulus, angle, off, end, county, lax.axis_index("gy"), len_y)
    coef_x = link_coefs(modulus, angle, off, end, countx, lax.axis_index("gx"), len_x)

    mxt = mx.T
    (my3, sp_y, lx, sx, edge_y, mxt, spread, edge_x, table, st, coef_y, coef_x) = lax.optimization_barrier(
        (my3, sp_y, lx, sx, edge_y, mxt, spread, edge_x, table, st, coef_y, coef_x)
    )

    turned = jax.ShapeDtypeStruct((2, nbx, nby * W, 2 * W), BF16)
    turned_spec = pl.BlockSpec((2, 1, nby * W, 2 * W), lambda a: (0, a, 0, 0))
    y_state_shape = jax.ShapeDtypeStruct((2, nbx, rows_y, W), F32)
    y_state_spec = pl.BlockSpec((2, 1, rows_y, W), lambda a: (0, a, 0, 0))
    y_piece_shape = jax.ShapeDtypeStruct((4, len_x), F32)
    y_piece_spec = pl.BlockSpec((4, W), lambda a: (0, a))
    field_spec = pl.BlockSpec((2, 1, W, len_y), lambda a: (0, 0, a, 0))
    keep_spec = pl.BlockSpec((2, W, len_y), lambda a: (0, a, 0))
    level_spec = lambda z: pl.BlockSpec((1, W, len_y), lambda a: (z, a, 0))
    turn_out = [turned, turned, y_state_shape] + [y_piece_shape] * county
    turn_specs = [turned_spec, turned_spec, y_state_spec] + [y_piece_spec] * county

    t_hi, t_lo, y_state, *y_pieces = pl.pallas_call(
        functools.partial(first_kernel, nby, county),
        grid=(nbx,),
        in_specs=[field_spec, field_spec, level_spec(depth - 1), whole(table.shape), whole(st.shape), SMEM, pl.BlockSpec(memory_space=pl.ANY)],
        out_specs=turn_specs,
        out_shape=turn_out,
        compiler_params=params(20),
        name="first",
    )(in_hbm(source_field), in_hbm(receiver_field), in_hbm(velocity_index), table, st, coef_y, my3)

    local = pl.pallas_call(
        functools.partial(local_kernel, nbx, nby),
        in_specs=[VMEM] * 6,
        out_specs=[VMEM] * 2,
        out_shape=[
            jax.ShapeDtypeStruct((2, nbx, 2 * W, len_y), F32),
            jax.ShapeDtypeStruct((2, rows_x, len_y), F32),
        ],
        scratch_shapes=[pltpu.VMEM((2 * W, len_y), BF16)] * 2,
        compiler_params=params(16),
        name="local",
    )

    link = pl.pallas_call(
        functools.partial(link_kernel, nbx, county, countx),
        in_specs=[VMEM] + [SMEM] * 2 + [VMEM] * (3 + county),
        out_specs=[VMEM] * (2 + countx),
        out_shape=[
            jax.ShapeDtypeStruct((2, nbx, 8, len_y), F32),
            jax.ShapeDtypeStruct((2, 8, 2 * len_x), F32),
        ] + [jax.ShapeDtypeStruct((4, len_y), F32)] * countx,
        compiler_params=params(8),
        name="link",
    )

    source_levels = {0: ("field", (source_field,))}
    kept = {}
    image = None
    for step in range(depth):
        w, x_local = local(t_hi, t_lo, y_state, my3, sp_y, lx)
        recv_y = exchange(y_pieces, "gy")
        x_state, ym, *x_pieces = link(x_local, coef_y, coef_x, sx, edge_y, mxt, *recv_y)
        recv_x = exchange(x_pieces, "gx")
        turn = step < depth - 1
        level_r = depth - 1 - step
        todo = [z for z in range(depth) if max(z - 1, depth - 1 - z) == step]
        plan = {
            "turn": turn,
            "keep": level_r - 1 > step,
            "images": [(z, None if z - 1 == step else source_levels[z][0], z != level_r) for z in todo],
        }
        args = [w, x_state, ym, coef_x, edge_y, spread, edge_x, table, *recv_x, in_hbm(velocity_index)]
        specs = [
            pl.BlockSpec((2, 1, 2 * W, len_y), lambda a: (0, a, 0, 0)),
            pl.BlockSpec((2, 1, 8, len_y), lambda a: (0, a, 0, 0)),
            pl.BlockSpec((2, 8, 2 * W), lambda a: (0, 0, a)),
            SMEM, whole(edge_y.shape), whole(spread.shape),
            pl.BlockSpec((1, 4, 2 * W), lambda a: (a, 0, 0)),
            whole(table.shape),
        ] + [whole((4, len_y))] * countx + [level_spec(step)]
        if turn:
            args += [in_hbm(velocity_index), st, coef_y]
            specs += [level_spec(depth - 2 - step), whole(st.shape), SMEM]
        for z, how, has_r in plan["images"]:
            if how == "split":
                args += [in_hbm(x) for x in source_levels[z][1]]
                specs += [pl.BlockSpec((1, 1, nby * W, 2 * W), lambda a: (0, a, 0, 0))] * 2
            elif how == "field":
                args += [in_hbm(x) for x in source_levels[z][1]]
                specs += [field_spec]
            if has_r:
                args += [in_hbm(kept[z])]
                specs += [keep_spec]
        if turn:
            shapes, out_specs = list(turn_out), list(turn_specs)
        else:
            shapes = [pltpu.HBM(source_field.shape, F32)] * 2
            out_specs = [field_spec] * 2
        if plan["keep"]:
            shapes.append(pltpu.HBM((2, len_x, len_y), F32))
            out_specs.append(keep_spec)
        aliases, scratch = {}, []
        if todo:
            if image is not None:
                aliases = {len(args): len(shapes)}
                args += [in_hbm(image)]
                specs += [pl.BlockSpec(memory_space=pl.ANY)]
            shapes.append(pltpu.HBM((depth, len_x, len_y), F32))
            out_specs.append(pl.BlockSpec(memory_space=pl.ANY))
            scratch = [pltpu.VMEM((len(todo), 2, W, len_y), F32), pltpu.SemaphoreType.DMA((len(todo), 2))]
        plan["alias"] = bool(aliases)
        outs = pl.pallas_call(
            functools.partial(post_kernel, plan, nby, county, countx),
            grid=(nbx,),
            in_specs=specs,
            out_specs=out_specs,
            out_shape=shapes,
            scratch_shapes=scratch,
            input_output_aliases=aliases,
            compiler_params=params(20),
            name="post",
        )(*args)
        outs = list(outs)
        if turn:
            t_hi, t_lo, y_state, *y_pieces = outs[: 3 + county]
            outs = outs[3 + county :]
            source_levels[step + 1] = ("split", (t_hi, t_lo))
        else:
            source, receiver = outs[:2]
            outs = outs[2:]
        if plan["keep"]:
            kept[level_r] = outs.pop(0)
        if todo:
            image = outs.pop(0)
    return image, source, receiver


def solution(mesh):
    placed = (
        P(None, None, "gx", "gy"),
        P(None, None, "gx", "gy"),
        P(None, "gx", "gy"),
        P(),
        P(),
        P(),
        P(),
    )
    return jax.shard_map(
        on_device,
        mesh=mesh,
        in_specs=placed,
        out_specs=(P(None, "gx", "gy"), P(None, None, "gx", "gy"), P(None, None, "gx", "gy")),
        check_vma=False,
    )
```

```python
import functools

import jax
import jax.numpy as jnp
import numpy as np
from jax import lax
from jax.experimental import pallas as pl
from jax.experimental.pallas import tpu as pltpu
from jax.sharding import PartitionSpec as P

PHASE_UNIT = 0.05
W = 128
F32 = jnp.float32
BF16 = jnp.bfloat16
HIGHEST = lax.Precision.HIGHEST
MIB = 1024 * 1024


def complex_mul(a, b):
    return (a[0] * b[0] - a[1] * b[1], a[0] * b[1] + a[1] * b[0])


def root_powers(modulus, angle, exponent):
    k = exponent.astype(F32)
    coarse = jnp.round(angle * 512.0)
    fine = angle - coarse * (1.0 / 512.0)
    steps = k * coarse
    turns = jnp.round(steps * np.float32(1.0 / 512.0 / (2.0 * np.pi)))
    spin = (steps * (1.0 / 512.0) - turns * 6.28125) - turns * np.float32(2.0 * np.pi - 6.28125)
    spin = spin + k * fine
    magnitude = jnp.exp(jnp.log(modulus) * k)
    return (magnitude * jnp.cos(spin), magnitude * jnp.sin(spin))


def sweep_factors(modulus, angle):
    sin, cos = jnp.sin(angle), jnp.cos(angle)
    gap = (1.0 - modulus) * (1.0 + modulus)
    re, im = modulus * cos, modulus * sin
    den_re, den_im = gap + 2.0 * im * im, -2.0 * re * im
    den_sq = den_re * den_re + den_im * den_im
    inv = (den_re / den_sq, -den_im / den_sq)
    diag = (re * re - im * im + gap * gap * inv[0], -2.0 * re * im + gap * gap * inv[1])
    root_inv = (re / (modulus * modulus), -im / (modulus * modulus))
    off = complex_mul((0.0 * im, 2.0 * gap * im), complex_mul(root_inv, inv))
    end = (-gap * gap * inv[0], -gap * gap * inv[1])
    return diag, off, end


def real_rows(pair):
    re, im = pair
    rows, n = re.shape
    nb = n // W
    first = jnp.stack([re.reshape(rows, nb, W), -im.reshape(rows, nb, W)], axis=2)
    second = jnp.stack([im.reshape(rows, nb, W), re.reshape(rows, nb, W)], axis=2)
    return jnp.stack([first, second], axis=1).reshape(2 * rows, 2 * n)


def spread_rows(pair):
    re, im = pair
    rows, n = re.shape
    nb = n // W
    first = jnp.stack([re.reshape(rows, nb, W), im.reshape(rows, nb, W)], axis=2)
    second = jnp.stack([-im.reshape(rows, nb, W), re.reshape(rows, nb, W)], axis=2)
    return jnp.stack([first, second], axis=1).reshape(2 * rows, 2 * n)


def pad_rows(x, rows):
    return jnp.pad(x, ((0, rows - x.shape[0]), (0, 0)))


def halves(x):
    hi = x.astype(BF16)
    return hi, (x - hi.astype(F32)).astype(BF16)


def rounded_halves(x):
    hi = lax.reduce_precision(x, exponent_bits=8, mantissa_bits=7)
    return hi.astype(BF16), (x - hi).astype(BF16)


def state_exponents(length):
    nb = length // W
    m = np.arange(length)
    rows, masks = [], []
    for b in range(nb):
        rows += [b * W - 1 - m, m - (b + 1) * W]
        masks += [m < b * W, m >= (b + 1) * W]
    rows += [length - 1 - m, m]
    masks += [m >= 0, m >= 0]
    return np.maximum(np.stack(rows), 0).astype(np.int32), np.stack(masks)


def state_matrix(modulus, angle, length):
    exps, masks = state_exponents(length)
    re, im = root_powers(modulus, angle, jnp.asarray(exps))
    masks = jnp.asarray(masks)
    return real_rows((jnp.where(masks, re, 0.0), jnp.where(masks, im, 0.0)))


def partner(mine, slot, count, way):
    if count & (count - 1) == 0:
        return mine ^ slot
    return (mine + way * slot) % count


def exchange(pieces, axis):
    count = len(pieces)
    got = [pieces[0]]
    for s in range(1, count):
        pairs = [(d, partner(d, s, count, 1)) for d in range(count)]
        got.append(lax.ppermute(pieces[s], axis, pairs))
    return got


def link_coefs(modulus, angle, off, end, count, mine, length):
    slots = np.arange(count, dtype=np.int32)
    root = (modulus * jnp.cos(angle), modulus * jnp.sin(angle))
    one = jnp.ones((count,), F32)
    zero = jnp.zeros((count,), F32)

    def factors(other):
        far = root_powers(modulus, angle, length * (2 * count - 2 - mine - other))
        near = root_powers(modulus, angle, length * jnp.maximum(jnp.abs(other - mine) - 1, 0))
        return near, complex_mul(end, far)

    other = partner(mine, slots, count, 1)
    near, tail = factors(other)
    head = complex_mul(complex_mul(off, root), near)
    before = other < mine
    send_f = (jnp.where(before, tail[0], one), jnp.where(before, tail[1], zero))
    send_b = (jnp.where(before, head[0], zero), jnp.where(before, head[1], zero))
    other = partner(mine, slots, count, -1)
    near, tail = factors(other)
    before, after = other < mine, other > mine
    recv_f = (jnp.where(before, near[0], zero), jnp.where(before, near[1], zero))
    recv_b = (jnp.where(after, one, tail[0]), jnp.where(after, zero, tail[1]))
    return jnp.stack([*send_f, *send_b, *recv_f, *recv_b], axis=1)


def split3(x, first):
    hi, lo = halves(x)
    return jnp.concatenate([hi, lo, hi] if first else [hi, hi, lo], axis=0)


def nt(a, b):
    return lax.dot_general(a, b, (((1,), (1,)), ((), ())), preferred_element_type=F32)


def tn(a, b):
    return lax.dot_general(a, b, (((0,), (0,)), ((), ())), preferred_element_type=F32)


def nn(a, b):
    return lax.dot_general(a, b, (((1,), (0,)), ((), ())), preferred_element_type=F32)


def lookup(table, index):
    chunks = table.shape[0]
    out = None
    for c in range(chunks):
        row = jnp.broadcast_to(table[c : c + 1, :], index.shape)
        here = jnp.clip(index - c * W, 0, W - 1) if chunks > 1 else index
        got = jnp.take_along_axis(row, here, axis=1, mode="promise_in_bounds")
        out = got if out is None else jnp.where(index >= c * W, got, out)
    return out


def weigh(coef, row, col, pair):
    cr, ci = coef[row, col], coef[row, col + 1]
    return (cr * pair[0] - ci * pair[1], cr * pair[1] + ci * pair[0])


def add_pair(a, b):
    return b if a is None else (a[0] + b[0], a[1] + b[1])


def gather_entries(coef, recv, count, chain):
    first = second = None
    for e in range(count):
        pair = (recv[e][2 * chain : 2 * chain + 1, :], recv[e][2 * chain + 1 : 2 * chain + 2, :])
        first = add_pair(first, weigh(coef, e, 4, pair))
        second = add_pair(second, weigh(coef, e, 6, pair))
    return first, second


def write_pieces(coef, pieces, count, chain, f_pair, b_pair):
    for e in range(count):
        out = add_pair(weigh(coef, e, 0, f_pair), weigh(coef, e, 2, b_pair))
        pieces[e][2 * chain : 2 * chain + 1, :] = out[0]
        pieces[e][2 * chain + 1 : 2 * chain + 2, :] = out[1]


def put_turned(t_hi, t_lo, chain, a, b, pair):
    for part in range(2):
        hi, lo = halves(pair[part])
        t_hi[chain, a, b * W : (b + 1) * W, part * W : (part + 1) * W] = hi
        t_lo[chain, a, b * W : (b + 1) * W, part * W : (part + 1) * W] = lo


def add_states(acc, t_hi, t_lo, st, a, b):
    rows = slice(b * W, (b + 1) * W)
    high = jnp.concatenate([t_hi[0, a, rows, :], t_hi[1, a, rows, :]], axis=0)
    low = jnp.concatenate([t_lo[0, a, rows, :], t_lo[1, a, rows, :]], axis=0)
    part = nn(jnp.concatenate([high, low], axis=1), st[b])
    return part if acc is None else acc + part


def put_states(acc, coef_y, y_state, y_pieces, nby, county, a):
    half = acc.shape[1] // 2
    rows = y_state.shape[2]
    turned = acc.T
    both = turned[:rows] + turned[half : half + rows]
    d = 4 * nby
    for chain in range(2):
        total = both[:, chain * W : (chain + 1) * W]
        y_state[chain, a] = total
        places = [ref.at[:, a * W : (a + 1) * W] for ref in y_pieces]
        write_pieces(
            coef_y, places, county, chain,
            (total[d : d + 1], total[d + 1 : d + 2]), (total[d + 2 : d + 3], total[d + 3 : d + 4]),
        )


def first_kernel(nby, county, src, rec, idx, table, st, coef_y, early, t_hi, t_lo, y_state, *y_pieces):
    acc = None
    for b in range(nby):
        lanes = slice(b * W, (b + 1) * W)
        put_turned(t_hi, t_lo, 0, 0, b, (src[0, 0, :, lanes], src[1, 0, :, lanes]))
        index = idx[0, :, lanes]
        cos, sin = lookup(table[0], index), lookup(table[1], index)
        put_turned(t_hi, t_lo, 1, 0, b, complex_mul((rec[0, 0, :, lanes], -rec[1, 0, :, lanes]), (cos, sin)))
        acc = add_states(acc, t_hi, t_lo, st, 0, b)
    put_states(acc, coef_y, y_state, y_pieces, nby, county, 0)


def local_kernel(nbx, nby, levels, t_hi, t_lo, y_state, my3, sp_y, lx, *refs):
    count = len(levels)
    far, (w_out, x_state), near = refs[:count], refs[count : count + 2], refs[count + 2 : 2 * count + 2]
    vx_hi, vx_lo, sems = refs[2 * count + 2 :]
    copies = []
    for n, level in enumerate(levels):
        source = far[n] if level is None else far[n].at[level]
        copies.append(pltpu.make_async_copy(source, near[n], sems.at[n]))
        copies[-1].start()
    x_state[...] = jnp.zeros_like(x_state)

    def block(i, carry):
        c, a = i // nbx, i % nbx
        state = y_state[c, a]
        for j in range(0, nby, 2):
            rows = slice(j * W, (j + 2) * W)
            high, low = t_hi[c, a, rows, :], t_lo[c, a, rows, :]
            main = nn(jnp.concatenate([high, low, high], axis=1), my3[...])
            for b in (j, j + 1):
                v = main[(b - j) * W : (b - j + 1) * W] + tn(split3(state[4 * b : 4 * b + 4, :], True), sp_y[...])
                hi, lo = halves(v)
                for part in range(2):
                    at = slice(part * W, (part + 1) * W)
                    vx_hi[at, b * W : (b + 1) * W] = hi[:, at]
                    vx_lo[at, b * W : (b + 1) * W] = lo[:, at]
        left = lx[a]
        for j in range(0, nby, 2):
            lanes = slice(j * W, (j + 2) * W)
            high, low = vx_hi[:, lanes], vx_lo[:, lanes]
            out = nn(left, jnp.concatenate([high, low, high], axis=0))
            w_out[c, a, :, lanes] = out[: 2 * W]
            x_state[c, :, lanes] += out[2 * W :]
        return carry

    lax.fori_loop(0, 2 * nbx, block, 0)
    for copy in copies:
        copy.wait()


def link_kernel(
    nbx, county, countx, x_local, coef_y, coef_x, sx, edge, mxt, *refs
):
    recv_y, (x_state, ym), x_pieces = refs[:county], refs[county : county + 2], refs[county + 2 :]
    for chain in range(2):
        (fr, fi), (br, bi) = gather_entries(coef_y, recv_y, county, chain)
        cols = []
        for a in range(nbx):
            lanes = slice(a * W, (a + 1) * W)
            top = jnp.concatenate([fr[:, lanes], fi[:, lanes]], axis=1)
            top2 = jnp.concatenate([-fi[:, lanes], fr[:, lanes]], axis=1)
            bot = jnp.concatenate([br[:, lanes], bi[:, lanes]], axis=1)
            bot2 = jnp.concatenate([-bi[:, lanes], br[:, lanes]], axis=1)
            cols.append(jnp.concatenate([top, top2, bot, bot2, jnp.zeros((4, 2 * W), F32)], axis=0))
        gain = None
        for a in range(nbx):
            ym[chain, :, 2 * W * a : 2 * W * (a + 1)] = lax.dot_general(
                cols[a], mxt[...], (((1,), (0,)), ((), ())), precision=HIGHEST, preferred_element_type=F32
            )
            part = lax.dot_general(
                sx[:, 2 * W * a : 2 * W * (a + 1)], cols[a], (((1,), (1,)), ((), ())),
                precision=HIGHEST, preferred_element_type=F32,
            )
            gain = part if gain is None else gain + part
        total = x_local[chain]
        for s in range(4):
            total = total + gain[:, s : s + 1] * edge[s : s + 1, :]
        for a in range(nbx):
            x_state[chain, a, 0:4, :] = total[4 * a : 4 * a + 4, :]
            x_state[chain, a, 4:8, :] = jnp.zeros((4, total.shape[1]), F32)
        d = 4 * nbx
        write_pieces(
            coef_x, x_pieces, countx, chain,
            (total[d : d + 1], total[d + 1 : d + 2]), (total[d + 2 : d + 3], total[d + 3 : d + 4]),
        )


def post_kernel(plan, nbx, nby, county, countx, *refs):
    refs = list(refs)
    take = lambda: refs.pop(0)
    w_in, x_state, ym, coef_x, edge, sp_x, sp_dev, table = (take() for _ in range(8))
    recv_x = [take() for _ in range(countx)]
    idx_s = take()
    idx_r, st, coef_y = (take(), take(), take()) if plan["turn"] else (None,) * 3
    olds = [{"s": (take(), take()) if z[1] == "split" else take() if z[1] == "field" else None,
             "r": take() if z[2] else None} for z in plan["images"]]
    if plan["alias"]:
        take()
    if plan["turn"]:
        t_hi, t_lo, y_state = (take() for _ in range(3))
        y_pieces = [take() for _ in range(county)]
    else:
        src_out, rec_out = take(), take()
    keep_out = take() if plan["keep"] else None
    image = take() if plan["images"] else None
    src_part, rec_part = (None, None) if plan["turn"] else (take(), take())
    keep_part = take() if plan["keep"] else None
    image_part = take() if plan["images"] else None
    sems = take()
    copies = []

    def send(part, out):
        copies.append(pltpu.make_async_copy(part, out, sems.at[len(copies)]))
        copies[-1].start()

    entries = [gather_entries(coef_x, recv_x, countx, chain) for chain in range(2)]
    for a in range(nbx):
        place = slice(a * W, (a + 1) * W)
        acc = None
        lefts, rights = [], []
        for chain in range(2):
            first, second = entries[chain]
            right = jnp.concatenate([x_state[chain, a, 0:4, :], *first, *second, edge[0:4, :]], axis=0)
            left = jnp.concatenate(
                [sp_x[...], sp_dev[a], ym[chain, 0:4, 2 * W * a : 2 * W * (a + 1)]], axis=0
            )
            rights.append(split3(right, False))
            lefts.append(split3(left, True))
        for b in range(nby):
            lanes = slice(b * W, (b + 1) * W)
            if b % 2 == 0:
                wide = slice(b * W, min(b + 2, nby) * W)
                fixes = [tn(lefts[chain], rights[chain][:, wide]) for chain in range(2)]
            fields = []
            for chain in range(2):
                u = w_in[chain, a, :, lanes] + fixes[chain][:, b % 2 * W : (b % 2 + 1) * W]
                fields.append((u[:W], u[W:]))
            index = idx_s[place, lanes]
            source = complex_mul(fields[0], (lookup(table[0], index), lookup(table[1], index)))
            back = fields[1]
            if plan["turn"]:
                put_turned(t_hi, t_lo, 0, a, b, source)
                index = idx_r[place, lanes]
                turn = (lookup(table[0], index), lookup(table[1], index))
                put_turned(t_hi, t_lo, 1, a, b, complex_mul(back, turn))
                acc = add_states(acc, t_hi, t_lo, st, a, b)
            else:
                src_part[a, 0, :, lanes], src_part[a, 1, :, lanes] = source
                rec_part[a, 0, :, lanes], rec_part[a, 1, :, lanes] = back[0], -back[1]
            if keep_out is not None:
                keep_part[a, 0, :, lanes], keep_part[a, 1, :, lanes] = back
            for n, (old, (_, how, has_r)) in enumerate(zip(olds, plan["images"])):
                if how == "split":
                    hi, lo = old["s"]
                    rows = slice(b * W, (b + 1) * W)
                    s = [hi[a, rows, p * W : (p + 1) * W].astype(F32) + lo[a, rows, p * W : (p + 1) * W].astype(F32)
                         for p in range(2)]
                elif how == "field":
                    s = (old["s"][0, 0, place, lanes], old["s"][1, 0, place, lanes])
                else:
                    s = source
                r = (old["r"][0, place, lanes], old["r"][1, place, lanes]) if has_r else back
                image_part[n, a, :, lanes] = s[0] * r[0] - s[1] * r[1]
        if plan["turn"]:
            put_states(acc, coef_y, y_state, y_pieces, nby, county, a)
        else:
            send(src_part.at[a], src_out.at[:, 0, place])
            send(rec_part.at[a], rec_out.at[:, 0, place])
        if plan["keep"]:
            send(keep_part.at[a], keep_out.at[:, place])
        for n, (z, _, _) in enumerate(plan["images"]):
            send(image_part.at[n, a], image.at[z, place])
    for copy in copies:
        copy.wait()


def whole(shape):
    return pl.BlockSpec(shape, lambda *_: (0,) * len(shape))


SMEM = pl.BlockSpec(memory_space=pltpu.SMEM)
VMEM = pl.BlockSpec(memory_space=pltpu.VMEM)
ANY = pl.BlockSpec(memory_space=pl.ANY)


def in_hbm(x):
    return pltpu.with_memory_space_constraint(x, pltpu.HBM)


def params(mib):
    return pltpu.CompilerParams(vmem_limit_bytes=mib * MIB)


def on_device(source_field, receiver_field, velocity_index, slowness, freq_index, root_modulus, root_angle):
    depth, len_x, len_y = velocity_index.shape
    nbx, nby = len_x // W, len_y // W
    countx, county = lax.axis_size("gx"), lax.axis_size("gy")
    modulus, angle = root_modulus[0], root_angle[0]
    diag, off, end = sweep_factors(modulus, angle)

    entries = slowness.shape[0]
    chunks = -(-entries // W)
    rate = freq_index.astype(F32)[0] * PHASE_UNIT
    phase = jnp.pad(rate * slowness, (0, chunks * W - entries)).reshape(chunks, W)
    table = jnp.stack([jnp.cos(phase), jnp.sin(phase)])

    at = np.arange(W)
    dist = np.abs(at[:, None] - at[None, :]).astype(np.int32)
    pw = root_powers(modulus, angle, jnp.asarray(dist))
    pw = complex_mul(off, pw)
    on = jnp.asarray(dist == 0)
    mr, mi = jnp.where(on, diag[0], pw[0]), jnp.where(on, diag[1], pw[1])
    my = jnp.concatenate([jnp.concatenate([mr, mi], 1), jnp.concatenate([-mi, mr], 1)], 0)
    mx = jnp.concatenate([jnp.concatenate([mr, -mi], 1), jnp.concatenate([mi, mr], 1)], 0)
    my_hi, my_lo = rounded_halves(my)
    mx_hi, mx_lo = rounded_halves(mx)

    rows_y = -(-(4 * nby + 4) // 16) * 16
    rows_x = -(-(4 * nbx + 4) // 16) * 16
    st_hi, st_lo = rounded_halves(pad_rows(state_matrix(modulus, angle, len_y), -(-rows_y // 64) * 64))
    st = jnp.concatenate([jnp.concatenate([st_hi, st_lo], axis=0), jnp.concatenate([st_hi, 0 * st_lo], axis=0)], axis=1)
    st = st.reshape(st.shape[0], 2, nby, 2 * W).transpose(2, 1, 3, 0).reshape(nby, 4 * W, st.shape[0])
    sx = pad_rows(state_matrix(modulus, angle, len_x), rows_x)
    sx_hi, sx_lo = rounded_halves(sx)
    lx = jnp.concatenate([
        jnp.broadcast_to(jnp.concatenate([mx_hi, mx_hi, mx_lo], axis=1)[None], (nbx, 2 * W, 6 * W)),
        jnp.concatenate([x.reshape(rows_x, nbx, 2 * W).transpose(1, 0, 2) for x in (sx_hi, sx_hi, sx_lo)], axis=2),
    ], axis=1)
    my3 = jnp.concatenate([my_hi, my_hi, my_lo], axis=0)

    near = complex_mul(off, root_powers(modulus, angle, jnp.asarray(np.stack([at + 1, W - at]).astype(np.int32))))
    spread = spread_rows(near)
    sp_hi, sp_lo = rounded_halves(spread)
    sp_y = jnp.concatenate([sp_hi, sp_hi, sp_lo], axis=0)

    def edges(length):
        m = np.arange(length)
        ahead = complex_mul(off, root_powers(modulus, angle, jnp.asarray((m + 1).astype(np.int32))))
        behind = root_powers(modulus, angle, jnp.asarray((length - 1 - m).astype(np.int32)))
        return jnp.stack([ahead[0], behind[0]]), jnp.stack([ahead[1], behind[1]])

    edge_x = spread_rows(edges(len_x)).reshape(4, nbx, 2 * W).transpose(1, 0, 2)
    er, ei = edges(len_y)
    edge_y = jnp.concatenate([jnp.stack([er, ei], axis=1).reshape(4, len_y), jnp.zeros((4, len_y), F32)], axis=0)

    coef_y = link_coefs(modulus, angle, off, end, county, lax.axis_index("gy"), len_y)
    coef_x = link_coefs(modulus, angle, off, end, countx, lax.axis_index("gx"), len_x)

    mxt = mx.T
    (my3, sp_y, lx, sx, edge_y, mxt, spread, edge_x, table, st, coef_y, coef_x) = lax.optimization_barrier(
        (my3, sp_y, lx, sx, edge_y, mxt, spread, edge_x, table, st, coef_y, coef_x)
    )

    turned = jax.ShapeDtypeStruct((2, nbx, nby * W, 2 * W), BF16)
    turned_spec = pl.BlockSpec((2, 1, nby * W, 2 * W), lambda a: (0, a, 0, 0))
    y_state_shape = jax.ShapeDtypeStruct((2, nbx, rows_y, W), F32)
    y_state_spec = pl.BlockSpec((2, 1, rows_y, W), lambda a: (0, a, 0, 0))
    y_piece_shape = jax.ShapeDtypeStruct((4, len_x), F32)
    y_piece_spec = pl.BlockSpec((4, W), lambda a: (0, a))
    field_spec = pl.BlockSpec((2, 1, W, len_y), lambda a: (0, 0, a, 0))
    level_spec = lambda z: pl.BlockSpec((1, W, len_y), lambda a: (z, a, 0))
    turn_out = [turned, turned, y_state_shape] + [y_piece_shape] * county
    turn_specs = [turned_spec, turned_spec, y_state_spec] + [y_piece_spec] * county

    t_hi, t_lo, y_state, *y_pieces = pl.pallas_call(
        functools.partial(first_kernel, nby, county),
        grid=(nbx,),
        in_specs=[field_spec, field_spec, level_spec(depth - 1), whole(table.shape), whole(st.shape), SMEM, ANY],
        out_specs=turn_specs,
        out_shape=turn_out,
        compiler_params=params(20),
        name="first",
    )(in_hbm(source_field), in_hbm(receiver_field), in_hbm(velocity_index), table, st, coef_y, my3)

    def local(t_hi, t_lo, y_state, ahead):
        shapes = [x.shape if level is None else x.shape[1:] for x, level in ahead]
        return pl.pallas_call(
            functools.partial(local_kernel, nbx, nby, tuple(level for _, level in ahead)),
            in_specs=[VMEM] * 6 + [ANY] * len(ahead),
            out_specs=[VMEM] * (2 + len(ahead)),
            out_shape=[
                jax.ShapeDtypeStruct((2, nbx, 2 * W, len_y), F32),
                jax.ShapeDtypeStruct((2, rows_x, len_y), F32),
            ] + [jax.ShapeDtypeStruct(shape, x.dtype) for (x, _), shape in zip(ahead, shapes)],
            scratch_shapes=[pltpu.VMEM((2 * W, len_y), BF16)] * 2 + [pltpu.SemaphoreType.DMA((len(ahead),))],
            compiler_params=params(8),
            name="local",
        )(t_hi, t_lo, y_state, my3, sp_y, lx, *[in_hbm(x) for x, _ in ahead])

    link = pl.pallas_call(
        functools.partial(link_kernel, nbx, county, countx),
        in_specs=[VMEM] + [SMEM] * 2 + [VMEM] * (3 + county),
        out_specs=[VMEM] * (2 + countx),
        out_shape=[
            jax.ShapeDtypeStruct((2, nbx, 8, len_y), F32),
            jax.ShapeDtypeStruct((2, 8, 2 * len_x), F32),
        ] + [jax.ShapeDtypeStruct((4, len_y), F32)] * countx,
        compiler_params=params(8),
        name="link",
    )

    source_levels = {0: ("field", (source_field,))}
    kept = {}
    image = None
    for step in range(depth):
        turn = step < depth - 1
        level_r = depth - 1 - step
        todo = [z for z in range(depth) if max(z - 1, depth - 1 - z) == step]
        plan = {
            "turn": turn,
            "keep": level_r - 1 > step,
            "images": [(z, None if z - 1 == step else source_levels[z][0], z != level_r) for z in todo],
            "alias": bool(todo) and image is not None,
        }
        ahead = [(velocity_index, step)] + ([(velocity_index, depth - 2 - step)] if turn else [])
        for z, how, has_r in plan["images"]:
            if how == "split":
                ahead += [(x, 0) for x in source_levels[z][1]]
            elif how == "field":
                ahead += [(x, None) for x in source_levels[z][1]]
            if has_r:
                ahead += [(kept[z], None)]
        w, x_local, *fetched = local(t_hi, t_lo, y_state, ahead)
        recv_y = exchange(y_pieces, "gy")
        x_state, ym, *x_pieces = link(x_local, coef_y, coef_x, sx, edge_y, mxt, *recv_y)
        recv_x = exchange(x_pieces, "gx")
        args = [w, x_state, ym, coef_x, edge_y, spread, edge_x, table, *recv_x, fetched.pop(0)]
        specs = [VMEM] * 3 + [SMEM] + [VMEM] * (5 + countx)
        if turn:
            args += [fetched.pop(0), st, coef_y]
            specs += [VMEM, VMEM, SMEM]
        args += fetched
        specs += [VMEM] * len(fetched)
        aliases, scratch, sends = {}, [], 0
        if turn:
            shapes, out_specs = list(turn_out), [VMEM] * len(turn_out)
        else:
            shapes = [pltpu.HBM(source_field.shape, F32)] * 2
            out_specs = [ANY] * 2
            scratch += [pltpu.VMEM((nbx, 2, W, len_y), F32)] * 2
            sends += 2
        if plan["keep"]:
            shapes.append(pltpu.HBM((2, len_x, len_y), F32))
            out_specs.append(ANY)
            scratch += [pltpu.VMEM((nbx, 2, W, len_y), F32)]
            sends += 1
        if todo:
            if plan["alias"]:
                aliases = {len(args): len(shapes)}
                args += [in_hbm(image)]
                specs += [ANY]
            shapes.append(pltpu.HBM((depth, len_x, len_y), F32))
            out_specs.append(ANY)
            scratch += [pltpu.VMEM((len(todo), nbx, W, len_y), F32)]
            sends += len(todo)
        outs = pl.pallas_call(
            functools.partial(post_kernel, plan, nbx, nby, county, countx),
            in_specs=specs,
            out_specs=out_specs,
            out_shape=shapes,
            scratch_shapes=scratch + [pltpu.SemaphoreType.DMA((max(sends, 1) * nbx,))],
            input_output_aliases=aliases,
            compiler_params=params(20),
            name="post",
        )(*args)
        outs = list(outs)
        if turn:
            t_hi, t_lo, y_state, *y_pieces = outs[: 3 + county]
            outs = outs[3 + county :]
            source_levels[step + 1] = ("split", (t_hi, t_lo))
        else:
            source, receiver = outs[:2]
            outs = outs[2:]
        if plan["keep"]:
            kept[level_r] = outs.pop(0)
        if todo:
            image = outs.pop(0)
    return image, source, receiver


def solution(mesh):
    placed = (
        P(None, None, "gx", "gy"),
        P(None, None, "gx", "gy"),
        P(None, "gx", "gy"),
        P(),
        P(),
        P(),
        P(),
    )
    return jax.shard_map(
        on_device,
        mesh=mesh,
        in_specs=placed,
        out_specs=(P(None, "gx", "gy"), P(None, None, "gx", "gy"), P(None, None, "gx", "gy")),
        check_vma=False,
    )
```

```python
import functools

import jax
import jax.numpy as jnp
import numpy as np
from jax import lax
from jax.experimental import pallas as pl
from jax.experimental.pallas import tpu as pltpu
from jax.sharding import PartitionSpec as P

PHASE_UNIT = 0.05
W = 128
F32 = jnp.float32
BF16 = jnp.bfloat16
MIB = 1024 * 1024


def complex_mul(a, b):
    return (a[0] * b[0] - a[1] * b[1], a[0] * b[1] + a[1] * b[0])


def root_powers(modulus, angle, exponent):
    k = exponent.astype(F32)
    coarse = jnp.round(angle * 512.0)
    fine = angle - coarse * (1.0 / 512.0)
    steps = k * coarse
    turns = jnp.round(steps * np.float32(1.0 / 512.0 / (2.0 * np.pi)))
    spin = (steps * (1.0 / 512.0) - turns * 6.28125) - turns * np.float32(2.0 * np.pi - 6.28125)
    spin = spin + k * fine
    magnitude = jnp.exp(jnp.log(modulus) * k)
    return (magnitude * jnp.cos(spin), magnitude * jnp.sin(spin))


def sweep_factors(modulus, angle):
    sin, cos = jnp.sin(angle), jnp.cos(angle)
    gap = (1.0 - modulus) * (1.0 + modulus)
    re, im = modulus * cos, modulus * sin
    den_re, den_im = gap + 2.0 * im * im, -2.0 * re * im
    den_sq = den_re * den_re + den_im * den_im
    inv = (den_re / den_sq, -den_im / den_sq)
    diag = (re * re - im * im + gap * gap * inv[0], -2.0 * re * im + gap * gap * inv[1])
    root_inv = (re / (modulus * modulus), -im / (modulus * modulus))
    off = complex_mul((0.0 * im, 2.0 * gap * im), complex_mul(root_inv, inv))
    end = (-gap * gap * inv[0], -gap * gap * inv[1])
    return diag, off, end


def real_rows(pair):
    re, im = pair
    rows, n = re.shape
    nb = n // W
    first = jnp.stack([re.reshape(rows, nb, W), -im.reshape(rows, nb, W)], axis=2)
    second = jnp.stack([im.reshape(rows, nb, W), re.reshape(rows, nb, W)], axis=2)
    return jnp.stack([first, second], axis=1).reshape(2 * rows, 2 * n)


def spread_rows(pair):
    re, im = pair
    rows, n = re.shape
    nb = n // W
    first = jnp.stack([re.reshape(rows, nb, W), im.reshape(rows, nb, W)], axis=2)
    second = jnp.stack([-im.reshape(rows, nb, W), re.reshape(rows, nb, W)], axis=2)
    return jnp.stack([first, second], axis=1).reshape(2 * rows, 2 * n)


def pad_rows(x, rows):
    return jnp.pad(x, ((0, rows - x.shape[0]), (0, 0)))


def halves(x):
    hi = x.astype(BF16)
    return hi, (x - hi.astype(F32)).astype(BF16)


def rounded_halves(x):
    hi = lax.reduce_precision(x, exponent_bits=8, mantissa_bits=7)
    return hi.astype(BF16), (x - hi).astype(BF16)


def state_exponents(length):
    nb = length // W
    m = np.arange(length)
    rows, masks = [], []
    for b in range(nb):
        rows += [b * W - 1 - m, m - (b + 1) * W]
        masks += [m < b * W, m >= (b + 1) * W]
    rows += [length - 1 - m, m]
    masks += [m >= 0, m >= 0]
    return np.maximum(np.stack(rows), 0).astype(np.int32), np.stack(masks)


def state_matrix(modulus, angle, length):
    exps, masks = state_exponents(length)
    re, im = root_powers(modulus, angle, jnp.asarray(exps))
    masks = jnp.asarray(masks)
    return real_rows((jnp.where(masks, re, 0.0), jnp.where(masks, im, 0.0)))


def partner(mine, slot, count, way):
    if count & (count - 1) == 0:
        return mine ^ slot
    return (mine + way * slot) % count


def exchange(pieces, axis):
    count = len(pieces)
    got = [pieces[0]]
    for s in range(1, count):
        pairs = [(d, partner(d, s, count, 1)) for d in range(count)]
        got.append(lax.ppermute(pieces[s], axis, pairs))
    return got


def link_coefs(modulus, angle, off, end, count, mine, length):
    slots = np.arange(count, dtype=np.int32)
    root = (modulus * jnp.cos(angle), modulus * jnp.sin(angle))
    one = jnp.ones((count,), F32)
    zero = jnp.zeros((count,), F32)

    def factors(other):
        far = root_powers(modulus, angle, length * (2 * count - 2 - mine - other))
        near = root_powers(modulus, angle, length * jnp.maximum(jnp.abs(other - mine) - 1, 0))
        return near, complex_mul(end, far)

    other = partner(mine, slots, count, 1)
    near, tail = factors(other)
    head = complex_mul(complex_mul(off, root), near)
    before = other < mine
    send_f = (jnp.where(before, tail[0], one), jnp.where(before, tail[1], zero))
    send_b = (jnp.where(before, head[0], zero), jnp.where(before, head[1], zero))
    other = partner(mine, slots, count, -1)
    near, tail = factors(other)
    before, after = other < mine, other > mine
    recv_f = (jnp.where(before, near[0], zero), jnp.where(before, near[1], zero))
    recv_b = (jnp.where(after, one, tail[0]), jnp.where(after, zero, tail[1]))
    return jnp.stack([*send_f, *send_b, *recv_f, *recv_b])


def split3(x, first):
    hi, lo = halves(x)
    return jnp.concatenate([hi, lo, hi] if first else [hi, hi, lo], axis=0)


def nt(a, b):
    return lax.dot_general(a, b, (((1,), (1,)), ((), ())), preferred_element_type=F32)


def tn(a, b):
    return lax.dot_general(a, b, (((0,), (0,)), ((), ())), preferred_element_type=F32)


def nn(a, b):
    return lax.dot_general(a, b, (((1,), (0,)), ((), ())), preferred_element_type=F32)


def lookup(table, index):
    chunks = table.shape[0]
    out = None
    for c in range(chunks):
        row = jnp.broadcast_to(table[c : c + 1, :], index.shape)
        here = jnp.clip(index - c * W, 0, W - 1) if chunks > 1 else index
        got = jnp.take_along_axis(row, here, axis=1, mode="promise_in_bounds")
        out = got if out is None else jnp.where(index >= c * W, got, out)
    return out


def weigh(coef, row, col, pair):
    cr, ci = coef[col, row], coef[col + 1, row]
    return (cr * pair[0] - ci * pair[1], cr * pair[1] + ci * pair[0])


def add_pair(a, b):
    return b if a is None else (a[0] + b[0], a[1] + b[1])


def gather_entries(coef, recv, count, chain):
    first = second = None
    for e in range(count):
        pair = (recv[e][2 * chain : 2 * chain + 1, :], recv[e][2 * chain + 1 : 2 * chain + 2, :])
        first = add_pair(first, weigh(coef, e, 4, pair))
        second = add_pair(second, weigh(coef, e, 6, pair))
    return first, second


def write_pieces(coef, pieces, count, chain, f_pair, b_pair):
    for e in range(count):
        out = add_pair(weigh(coef, e, 0, f_pair), weigh(coef, e, 2, b_pair))
        pieces[e][2 * chain : 2 * chain + 1, :] = out[0]
        pieces[e][2 * chain + 1 : 2 * chain + 2, :] = out[1]


def put_turned(t_hi, t_lo, chain, a, b, pair):
    for part in range(2):
        hi, lo = halves(pair[part])
        t_hi[chain, a, b * W : (b + 1) * W, part * W : (part + 1) * W] = hi
        t_lo[chain, a, b * W : (b + 1) * W, part * W : (part + 1) * W] = lo


def add_states(acc, t_hi, t_lo, st, a, b):
    rows = slice(b * W, (b + 1) * W)
    high = jnp.concatenate([t_hi[0, a, rows, :], t_hi[1, a, rows, :]], axis=0)
    low = jnp.concatenate([t_lo[0, a, rows, :], t_lo[1, a, rows, :]], axis=0)
    part = nn(jnp.concatenate([high, low], axis=1), st[b])
    return part if acc is None else acc + part


def put_states(acc, coef_y, y_state, y_pieces, nby, county, a):
    half = acc.shape[1] // 2
    rows = y_state.shape[2]
    turned = acc.T
    both = turned[:rows] + turned[half : half + rows]
    d = 4 * nby
    for chain in range(2):
        total = both[:, chain * W : (chain + 1) * W]
        y_state[chain, a] = total
        places = [ref.at[:, a * W : (a + 1) * W] for ref in y_pieces]
        write_pieces(
            coef_y, places, county, chain,
            (total[d : d + 1], total[d + 1 : d + 2]), (total[d + 2 : d + 3], total[d + 3 : d + 4]),
        )


def first_kernel(nby, county, src, rec, idx, table, st, coef_y, early, t_hi, t_lo, y_state, *y_pieces):
    acc = None
    for b in range(nby):
        lanes = slice(b * W, (b + 1) * W)
        put_turned(t_hi, t_lo, 0, 0, b, (src[0, 0, :, lanes], src[1, 0, :, lanes]))
        index = idx[0, :, lanes]
        cos, sin = lookup(table[0], index), lookup(table[1], index)
        put_turned(t_hi, t_lo, 1, 0, b, complex_mul((rec[0, 0, :, lanes], -rec[1, 0, :, lanes]), (cos, sin)))
        acc = add_states(acc, t_hi, t_lo, st, 0, b)
    put_states(acc, coef_y, y_state, y_pieces, nby, county, 0)


def local_kernel(nbx, nby, levels, t_hi, t_lo, y_state, my3, sp_y, lx, *refs):
    count = len(levels)
    far, (w_out, x_state), near = refs[:count], refs[count : count + 2], refs[count + 2 : 2 * count + 2]
    vx_hi, vx_lo, sems = refs[2 * count + 2 :]
    copies = []
    for n, level in enumerate(levels):
        source = far[n] if level is None else far[n].at[level]
        copies.append(pltpu.make_async_copy(source, near[n], sems.at[n]))
        copies[-1].start()
    x_state[...] = jnp.zeros_like(x_state)

    def block(i, carry):
        c, a = i // nbx, i % nbx
        state = y_state[c, a]
        for j in range(0, nby, 2):
            rows = slice(j * W, (j + 2) * W)
            high, low = t_hi[c, a, rows, :], t_lo[c, a, rows, :]
            main = nn(jnp.concatenate([high, low, high], axis=1), my3[...])
            for b in (j, j + 1):
                v = main[(b - j) * W : (b - j + 1) * W] + tn(split3(state[4 * b : 4 * b + 4, :], True), sp_y[...])
                hi, lo = halves(v)
                for part in range(2):
                    at = slice(part * W, (part + 1) * W)
                    vx_hi[at, b * W : (b + 1) * W] = hi[:, at]
                    vx_lo[at, b * W : (b + 1) * W] = lo[:, at]
        left = lx[a]
        for j in range(0, nby, 2):
            lanes = slice(j * W, (j + 2) * W)
            high, low = vx_hi[:, lanes], vx_lo[:, lanes]
            out = nn(left, jnp.concatenate([high, low, high], axis=0))
            w_out[c, a, :, lanes] = out[: 2 * W]
            x_state[c, :, lanes] += out[2 * W :]
        return carry

    lax.fori_loop(0, 2 * nbx, block, 0)
    for copy in copies:
        copy.wait()


def link_kernel(nbx, county, countx, x_local, coef_y, coef_x, sx3, edge, my3, *refs):
    recv_y, (x_state, ym), x_pieces = refs[:county], refs[county : county + 2], refs[county + 2 :]
    cols = []
    for chain in range(2):
        (fr, fi), (br, bi) = gather_entries(coef_y, recv_y, county, chain)
        rows = [(fr, fi), (-fi, fr), (br, bi), (-bi, br)]
        for a in range(nbx):
            lanes = slice(a * W, (a + 1) * W)
            cols.append(jnp.concatenate([jnp.concatenate([p[:, lanes], q[:, lanes]], axis=1) for p, q in rows]
                                        + [jnp.zeros((4, 2 * W), F32)], axis=0))
    hi, lo = halves(jnp.concatenate(cols, axis=0))
    swept = nn(jnp.concatenate([hi, lo, hi], axis=1), my3[...])
    for chain in range(2):
        for a in range(nbx):
            at = 8 * (chain * nbx + a)
            ym[chain, :, 2 * W * a : 2 * W * (a + 1)] = swept[at : at + 8]
    lines = jnp.concatenate(
        [jnp.concatenate(cols[chain * nbx : (chain + 1) * nbx], axis=1) for chain in range(2)], axis=0
    )
    hi, lo = halves(lines)
    gains = nt(sx3[...], jnp.concatenate([hi, lo, hi], axis=1))
    for chain in range(2):
        total = x_local[chain]
        for s in range(4):
            total = total + gains[:, 8 * chain + s : 8 * chain + s + 1] * edge[s : s + 1, :]
        for a in range(nbx):
            x_state[chain, a, 0:4, :] = total[4 * a : 4 * a + 4, :]
            x_state[chain, a, 4:8, :] = jnp.zeros((4, total.shape[1]), F32)
        d = 4 * nbx
        write_pieces(
            coef_x, x_pieces, countx, chain,
            (total[d : d + 1], total[d + 1 : d + 2]), (total[d + 2 : d + 3], total[d + 3 : d + 4]),
        )


def post_kernel(plan, nbx, nby, county, countx, *refs):
    refs = list(refs)
    take = lambda: refs.pop(0)
    w_in, x_state, ym, coef_x, edge, sp_x, sp_dev, table = (take() for _ in range(8))
    recv_x = [take() for _ in range(countx)]
    idx_s = take()
    idx_r, st, coef_y = (take(), take(), take()) if plan["turn"] else (None,) * 3
    olds = [{"s": (take(), take()) if z[1] == "split" else take() if z[1] == "field" else None,
             "r": take() if z[2] else None} for z in plan["images"]]
    if plan["alias"]:
        take()
    if plan["turn"]:
        t_hi, t_lo, y_state = (take() for _ in range(3))
        y_pieces = [take() for _ in range(county)]
    else:
        src_out, rec_out = take(), take()
    keep_out = take() if plan["keep"] else None
    image = take() if plan["images"] else None
    src_part, rec_part = (None, None) if plan["turn"] else (take(), take())
    keep_part = take() if plan["keep"] else None
    image_part = take() if plan["images"] else None
    sems = take()
    copies = []

    def send(part, out):
        copies.append(pltpu.make_async_copy(part, out, sems.at[len(copies)]))
        copies[-1].start()

    entries = [gather_entries(coef_x, recv_x, countx, chain) for chain in range(2)]
    step = 2 if nby % 2 == 0 else 1
    chunks = [(a, b) for a in range(nbx) for b in range(0, nby, step)]
    stacks = {}

    def correction(a, start):
        if a not in stacks:
            stacks[a] = []
            for chain in range(2):
                first, second = entries[chain]
                right = jnp.concatenate([x_state[chain, a, 0:4, :], *first, *second, edge[0:4, :]], axis=0)
                left = jnp.concatenate(
                    [sp_x[...], sp_dev[a], ym[chain, 0:4, 2 * W * a : 2 * W * (a + 1)]], axis=0
                )
                stacks[a].append((split3(left, True), split3(right, False)))
        return [tn(left, right[:, start * W : (start + step) * W]) for left, right in stacks[a]]

    def finish(a, b):
        nonlocal acc
        if plan["turn"]:
            acc = add_states(acc if b else None, t_hi, t_lo, st, a, b)
            if b == nby - 1:
                put_states(acc, coef_y, y_state, y_pieces, nby, county, a)

    acc, before = None, None
    coming = correction(*chunks[0])
    for n_chunk, (a, start) in enumerate(chunks):
        place = slice(a * W, (a + 1) * W)
        fixes = coming
        if n_chunk + 1 < len(chunks):
            coming = correction(*chunks[n_chunk + 1])
        for b in range(start, start + step):
            lanes = slice(b * W, (b + 1) * W)
            fields = []
            for chain in range(2):
                u = w_in[chain, a, :, lanes] + fixes[chain][:, (b - start) * W : (b - start + 1) * W]
                fields.append((u[:W], u[W:]))
            index = idx_s[place, lanes]
            source = complex_mul(fields[0], (lookup(table[0], index), lookup(table[1], index)))
            back = fields[1]
            if plan["turn"]:
                put_turned(t_hi, t_lo, 0, a, b, source)
                index = idx_r[place, lanes]
                turn = (lookup(table[0], index), lookup(table[1], index))
                put_turned(t_hi, t_lo, 1, a, b, complex_mul(back, turn))
            else:
                src_part[a, 0, :, lanes], src_part[a, 1, :, lanes] = source
                rec_part[a, 0, :, lanes], rec_part[a, 1, :, lanes] = back[0], -back[1]
            if keep_out is not None:
                keep_part[a, 0, :, lanes], keep_part[a, 1, :, lanes] = back
            for n, (old, (_, how, has_r)) in enumerate(zip(olds, plan["images"])):
                if how == "split":
                    hi, lo = old["s"]
                    rows = slice(b * W, (b + 1) * W)
                    s = [hi[a, rows, p * W : (p + 1) * W].astype(F32) + lo[a, rows, p * W : (p + 1) * W].astype(F32)
                         for p in range(2)]
                elif how == "field":
                    s = (old["s"][0, 0, place, lanes], old["s"][1, 0, place, lanes])
                else:
                    s = source
                r = (old["r"][0, place, lanes], old["r"][1, place, lanes]) if has_r else back
                image_part[n, a, :, lanes] = s[0] * r[0] - s[1] * r[1]
            if before is not None:
                finish(*before)
            before = (a, b)
        if start + step < nby:
            continue
        if not plan["turn"]:
            send(src_part.at[a], src_out.at[:, 0, place])
            send(rec_part.at[a], rec_out.at[:, 0, place])
        if plan["keep"]:
            send(keep_part.at[a], keep_out.at[:, place])
        for n, (z, _, _) in enumerate(plan["images"]):
            send(image_part.at[n, a], image.at[z, place])
    finish(*before)
    for copy in copies:
        copy.wait()


def whole(shape):
    return pl.BlockSpec(shape, lambda *_: (0,) * len(shape))


SMEM = pl.BlockSpec(memory_space=pltpu.SMEM)
VMEM = pl.BlockSpec(memory_space=pltpu.VMEM)
ANY = pl.BlockSpec(memory_space=pl.ANY)


def in_hbm(x):
    return pltpu.with_memory_space_constraint(x, pltpu.HBM)


def params(mib):
    return pltpu.CompilerParams(vmem_limit_bytes=mib * MIB)


def on_device(source_field, receiver_field, velocity_index, slowness, freq_index, root_modulus, root_angle):
    depth, len_x, len_y = velocity_index.shape
    nbx, nby = len_x // W, len_y // W
    countx, county = lax.axis_size("gx"), lax.axis_size("gy")
    modulus, angle = root_modulus[0], root_angle[0]
    diag, off, end = sweep_factors(modulus, angle)

    entries = slowness.shape[0]
    chunks = -(-entries // W)
    rate = freq_index.astype(F32)[0] * PHASE_UNIT
    phase = jnp.pad(rate * slowness, (0, chunks * W - entries)).reshape(chunks, W)
    table = jnp.stack([jnp.cos(phase), jnp.sin(phase)])

    at = np.arange(W)
    dist = np.abs(at[:, None] - at[None, :]).astype(np.int32)
    pw = root_powers(modulus, angle, jnp.asarray(dist))
    pw = complex_mul(off, pw)
    on = jnp.asarray(dist == 0)
    mr, mi = jnp.where(on, diag[0], pw[0]), jnp.where(on, diag[1], pw[1])
    my = jnp.concatenate([jnp.concatenate([mr, mi], 1), jnp.concatenate([-mi, mr], 1)], 0)
    mx = jnp.concatenate([jnp.concatenate([mr, -mi], 1), jnp.concatenate([mi, mr], 1)], 0)
    my_hi, my_lo = rounded_halves(my)
    mx_hi, mx_lo = rounded_halves(mx)

    rows_y = -(-(4 * nby + 4) // 16) * 16
    rows_x = -(-(4 * nbx + 4) // 16) * 16
    st_hi, st_lo = rounded_halves(pad_rows(state_matrix(modulus, angle, len_y), -(-rows_y // 64) * 64))
    st = jnp.concatenate([jnp.concatenate([st_hi, st_lo], axis=0), jnp.concatenate([st_hi, 0 * st_lo], axis=0)], axis=1)
    st = st.reshape(st.shape[0], 2, nby, 2 * W).transpose(2, 1, 3, 0).reshape(nby, 4 * W, st.shape[0])
    sx = pad_rows(state_matrix(modulus, angle, len_x), rows_x)
    sx_hi, sx_lo = rounded_halves(sx)
    lx = jnp.concatenate([
        jnp.broadcast_to(jnp.concatenate([mx_hi, mx_hi, mx_lo], axis=1)[None], (nbx, 2 * W, 6 * W)),
        jnp.concatenate([x.reshape(rows_x, nbx, 2 * W).transpose(1, 0, 2) for x in (sx_hi, sx_hi, sx_lo)], axis=2),
    ], axis=1)
    my3 = jnp.concatenate([my_hi, my_hi, my_lo], axis=0)

    near = complex_mul(off, root_powers(modulus, angle, jnp.asarray(np.stack([at + 1, W - at]).astype(np.int32))))
    spread = spread_rows(near)
    sp_hi, sp_lo = rounded_halves(spread)
    sp_y = jnp.concatenate([sp_hi, sp_hi, sp_lo], axis=0)

    def edges(length):
        m = np.arange(length)
        ahead = complex_mul(off, root_powers(modulus, angle, jnp.asarray((m + 1).astype(np.int32))))
        behind = root_powers(modulus, angle, jnp.asarray((length - 1 - m).astype(np.int32)))
        return jnp.stack([ahead[0], behind[0]]), jnp.stack([ahead[1], behind[1]])

    edge_x = spread_rows(edges(len_x)).reshape(4, nbx, 2 * W).transpose(1, 0, 2)
    er, ei = edges(len_y)
    edge_y = jnp.concatenate([jnp.stack([er, ei], axis=1).reshape(4, len_y), jnp.zeros((4, len_y), F32)], axis=0)

    coef_y = link_coefs(modulus, angle, off, end, county, lax.axis_index("gy"), len_y)
    coef_x = link_coefs(modulus, angle, off, end, countx, lax.axis_index("gx"), len_x)

    sx3 = jnp.concatenate([sx_hi, sx_hi, sx_lo], axis=1)
    (my3, sp_y, lx, sx3, edge_y, spread, edge_x, table, st, coef_y, coef_x) = lax.optimization_barrier(
        (my3, sp_y, lx, sx3, edge_y, spread, edge_x, table, st, coef_y, coef_x)
    )

    turned = jax.ShapeDtypeStruct((2, nbx, nby * W, 2 * W), BF16)
    turned_spec = pl.BlockSpec((2, 1, nby * W, 2 * W), lambda a: (0, a, 0, 0))
    y_state_shape = jax.ShapeDtypeStruct((2, nbx, rows_y, W), F32)
    y_state_spec = pl.BlockSpec((2, 1, rows_y, W), lambda a: (0, a, 0, 0))
    y_piece_shape = jax.ShapeDtypeStruct((4, len_x), F32)
    y_piece_spec = pl.BlockSpec((4, W), lambda a: (0, a))
    field_spec = pl.BlockSpec((2, 1, W, len_y), lambda a: (0, 0, a, 0))
    level_spec = lambda z: pl.BlockSpec((1, W, len_y), lambda a: (z, a, 0))
    turn_out = [turned, turned, y_state_shape] + [y_piece_shape] * county
    turn_specs = [turned_spec, turned_spec, y_state_spec] + [y_piece_spec] * county

    t_hi, t_lo, y_state, *y_pieces = pl.pallas_call(
        functools.partial(first_kernel, nby, county),
        grid=(nbx,),
        in_specs=[field_spec, field_spec, level_spec(depth - 1), whole(table.shape), whole(st.shape), SMEM, ANY],
        out_specs=turn_specs,
        out_shape=turn_out,
        compiler_params=params(20),
        name="first",
    )(in_hbm(source_field), in_hbm(receiver_field), in_hbm(velocity_index), table, st, coef_y, my3)

    def local(t_hi, t_lo, y_state, ahead):
        shapes = [x.shape if level is None else x.shape[1:] for x, level in ahead]
        return pl.pallas_call(
            functools.partial(local_kernel, nbx, nby, tuple(level for _, level in ahead)),
            in_specs=[VMEM] * 6 + [ANY] * len(ahead),
            out_specs=[VMEM] * (2 + len(ahead)),
            out_shape=[
                jax.ShapeDtypeStruct((2, nbx, 2 * W, len_y), F32),
                jax.ShapeDtypeStruct((2, rows_x, len_y), F32),
            ] + [jax.ShapeDtypeStruct(shape, x.dtype) for (x, _), shape in zip(ahead, shapes)],
            scratch_shapes=[pltpu.VMEM((2 * W, len_y), BF16)] * 2 + [pltpu.SemaphoreType.DMA((len(ahead),))],
            compiler_params=params(8),
            name="local",
        )(t_hi, t_lo, y_state, my3, sp_y, lx, *[in_hbm(x) for x, _ in ahead])

    link = pl.pallas_call(
        functools.partial(link_kernel, nbx, county, countx),
        in_specs=[VMEM] + [SMEM] * 2 + [VMEM] * (3 + county),
        out_specs=[VMEM] * (2 + countx),
        out_shape=[
            jax.ShapeDtypeStruct((2, nbx, 8, len_y), F32),
            jax.ShapeDtypeStruct((2, 8, 2 * len_x), F32),
        ] + [jax.ShapeDtypeStruct((4, len_y), F32)] * countx,
        compiler_params=params(8),
        name="link",
    )

    source_levels = {0: ("field", (source_field,))}
    kept = {}
    image = None
    for step in range(depth):
        turn = step < depth - 1
        level_r = depth - 1 - step
        todo = [z for z in range(depth) if max(z - 1, depth - 1 - z) == step]
        plan = {
            "turn": turn,
            "keep": level_r - 1 > step,
            "images": [(z, None if z - 1 == step else source_levels[z][0], z != level_r) for z in todo],
            "alias": bool(todo) and image is not None,
        }
        ahead = [(velocity_index, step)] + ([(velocity_index, depth - 2 - step)] if turn else [])
        for z, how, has_r in plan["images"]:
            if how == "split":
                ahead += [(x, 0) for x in source_levels[z][1]]
            elif how == "field":
                ahead += [(x, None) for x in source_levels[z][1]]
            if has_r:
                ahead += [(kept[z], None)]
        w, x_local, *fetched = local(t_hi, t_lo, y_state, ahead)
        recv_y = exchange(y_pieces, "gy")
        x_state, ym, *x_pieces = link(x_local, coef_y, coef_x, sx3, edge_y, my3, *recv_y)
        recv_x = exchange(x_pieces, "gx")
        args = [w, x_state, ym, coef_x, edge_y, spread, edge_x, table, *recv_x, fetched.pop(0)]
        specs = [VMEM] * 3 + [SMEM] + [VMEM] * (5 + countx)
        if turn:
            args += [fetched.pop(0), st, coef_y]
            specs += [VMEM, VMEM, SMEM]
        args += fetched
        specs += [VMEM] * len(fetched)
        aliases, scratch, sends = {}, [], 0
        if turn:
            shapes, out_specs = list(turn_out), [VMEM] * len(turn_out)
        else:
            shapes = [pltpu.HBM(source_field.shape, F32)] * 2
            out_specs = [ANY] * 2
            scratch += [pltpu.VMEM((nbx, 2, W, len_y), F32)] * 2
            sends += 2
        if plan["keep"]:
            shapes.append(pltpu.HBM((2, len_x, len_y), F32))
            out_specs.append(ANY)
            scratch += [pltpu.VMEM((nbx, 2, W, len_y), F32)]
            sends += 1
        if todo:
            if plan["alias"]:
                aliases = {len(args): len(shapes)}
                args += [in_hbm(image)]
                specs += [ANY]
            shapes.append(pltpu.HBM((depth, len_x, len_y), F32))
            out_specs.append(ANY)
            scratch += [pltpu.VMEM((len(todo), nbx, W, len_y), F32)]
            sends += len(todo)
        outs = pl.pallas_call(
            functools.partial(post_kernel, plan, nbx, nby, county, countx),
            in_specs=specs,
            out_specs=out_specs,
            out_shape=shapes,
            scratch_shapes=scratch + [pltpu.SemaphoreType.DMA((max(sends, 1) * nbx,))],
            input_output_aliases=aliases,
            compiler_params=params(20),
            name="post",
        )(*args)
        outs = list(outs)
        if turn:
            t_hi, t_lo, y_state, *y_pieces = outs[: 3 + county]
            outs = outs[3 + county :]
            source_levels[step + 1] = ("split", (t_hi, t_lo))
        else:
            source, receiver = outs[:2]
            outs = outs[2:]
        if plan["keep"]:
            kept[level_r] = outs.pop(0)
        if todo:
            image = outs.pop(0)
    return image, source, receiver


def solution(mesh):
    placed = (
        P(None, None, "gx", "gy"),
        P(None, None, "gx", "gy"),
        P(None, "gx", "gy"),
        P(),
        P(),
        P(),
        P(),
    )
    return jax.shard_map(
        on_device,
        mesh=mesh,
        in_specs=placed,
        out_specs=(P(None, "gx", "gy"), P(None, None, "gx", "gy"), P(None, None, "gx", "gy")),
        check_vma=False,
    )
```

```python
import functools

import jax
import jax.numpy as jnp
import numpy as np
from jax import lax
from jax.experimental import pallas as pl
from jax.experimental.pallas import tpu as pltpu
from jax.sharding import PartitionSpec as P

PHASE_UNIT = 0.05
W = 128
F32 = jnp.float32
BF16 = jnp.bfloat16
MIB = 1024 * 1024


def complex_mul(a, b):
    return (a[0] * b[0] - a[1] * b[1], a[0] * b[1] + a[1] * b[0])


def root_powers(modulus, angle, exponent):
    k = exponent.astype(F32)
    coarse = jnp.round(angle * 512.0)
    fine = angle - coarse * (1.0 / 512.0)
    steps = k * coarse
    turns = jnp.round(steps * np.float32(1.0 / 512.0 / (2.0 * np.pi)))
    spin = (steps * (1.0 / 512.0) - turns * 6.28125) - turns * np.float32(2.0 * np.pi - 6.28125)
    spin = spin + k * fine
    magnitude = jnp.exp(jnp.log(modulus) * k)
    return (magnitude * jnp.cos(spin), magnitude * jnp.sin(spin))


def sweep_factors(modulus, angle):
    sin, cos = jnp.sin(angle), jnp.cos(angle)
    gap = (1.0 - modulus) * (1.0 + modulus)
    re, im = modulus * cos, modulus * sin
    den_re, den_im = gap + 2.0 * im * im, -2.0 * re * im
    den_sq = den_re * den_re + den_im * den_im
    inv = (den_re / den_sq, -den_im / den_sq)
    diag = (re * re - im * im + gap * gap * inv[0], -2.0 * re * im + gap * gap * inv[1])
    root_inv = (re / (modulus * modulus), -im / (modulus * modulus))
    off = complex_mul((0.0 * im, 2.0 * gap * im), complex_mul(root_inv, inv))
    end = (-gap * gap * inv[0], -gap * gap * inv[1])
    return diag, off, end


def real_rows(pair):
    re, im = pair
    rows, n = re.shape
    nb = n // W
    first = jnp.stack([re.reshape(rows, nb, W), -im.reshape(rows, nb, W)], axis=2)
    second = jnp.stack([im.reshape(rows, nb, W), re.reshape(rows, nb, W)], axis=2)
    return jnp.stack([first, second], axis=1).reshape(2 * rows, 2 * n)


def spread_rows(pair):
    re, im = pair
    rows, n = re.shape
    nb = n // W
    first = jnp.stack([re.reshape(rows, nb, W), im.reshape(rows, nb, W)], axis=2)
    second = jnp.stack([-im.reshape(rows, nb, W), re.reshape(rows, nb, W)], axis=2)
    return jnp.stack([first, second], axis=1).reshape(2 * rows, 2 * n)


def pad_rows(x, rows):
    return jnp.pad(x, ((0, rows - x.shape[0]), (0, 0)))


def halves(x):
    hi = x.astype(BF16)
    return hi, (x - hi.astype(F32)).astype(BF16)


def rounded_halves(x):
    hi = lax.reduce_precision(x, exponent_bits=8, mantissa_bits=7)
    return hi.astype(BF16), (x - hi).astype(BF16)


def state_exponents(length):
    nb = length // W
    m = np.arange(length)
    rows, masks = [], []
    for b in range(nb):
        rows += [b * W - 1 - m, m - (b + 1) * W]
        masks += [m < b * W, m >= (b + 1) * W]
    rows += [length - 1 - m, m]
    masks += [m >= 0, m >= 0]
    return np.maximum(np.stack(rows), 0).astype(np.int32), np.stack(masks)


def state_matrix(modulus, angle, length):
    exps, masks = state_exponents(length)
    re, im = root_powers(modulus, angle, jnp.asarray(exps))
    masks = jnp.asarray(masks)
    return real_rows((jnp.where(masks, re, 0.0), jnp.where(masks, im, 0.0)))


def partner(mine, slot, count, way):
    if count & (count - 1) == 0:
        return mine ^ slot
    return (mine + way * slot) % count


def exchange(pieces, axis):
    count = len(pieces)
    got = [pieces[0]]
    for s in range(1, count):
        pairs = [(d, partner(d, s, count, 1)) for d in range(count)]
        got.append(lax.ppermute(pieces[s], axis, pairs))
    return got


def link_coefs(modulus, angle, off, end, count, mine, length):
    slots = np.arange(count, dtype=np.int32)
    row = np.arange(8)[:, None]
    other = jnp.where(row < 4, partner(mine, slots, count, 1)[None], partner(mine, slots, count, -1)[None])
    far = (row < 2) | (row >= 6)
    apart = jnp.where(far, 2 * count - 2 - mine - other, jnp.maximum(jnp.abs(other - mine) - 1, 0))
    power = root_powers(modulus, angle, length * apart)
    head = complex_mul(off, (modulus * jnp.cos(angle), modulus * jnp.sin(angle)))
    lead = (row == 2) | (row == 3)
    factor = [jnp.where(far, end[n], jnp.where(lead, head[n], 1.0 - n)) for n in range(2)]
    value = complex_mul(factor, power)
    real = row % 2 == 0
    used = jnp.where(row < 6, other < mine, other <= mine)
    return jnp.where(used, jnp.where(real, value[0], value[1]), jnp.where(far & real, 1.0, 0.0))


def split3(x, first):
    hi, lo = halves(x)
    return jnp.concatenate([hi, lo, hi] if first else [hi, hi, lo], axis=0)


def nt(a, b):
    return lax.dot_general(a, b, (((1,), (1,)), ((), ())), preferred_element_type=F32)


def tn(a, b):
    return lax.dot_general(a, b, (((0,), (0,)), ((), ())), preferred_element_type=F32)


def nn(a, b):
    return lax.dot_general(a, b, (((1,), (0,)), ((), ())), preferred_element_type=F32)


def lookup(table, index):
    chunks = table.shape[0]
    out = None
    for c in range(chunks):
        row = jnp.broadcast_to(table[c : c + 1, :], index.shape)
        here = jnp.clip(index - c * W, 0, W - 1) if chunks > 1 else index
        got = jnp.take_along_axis(row, here, axis=1, mode="promise_in_bounds")
        out = got if out is None else jnp.where(index >= c * W, got, out)
    return out


def weigh(coef, row, col, pair):
    cr, ci = coef[col, row], coef[col + 1, row]
    return (cr * pair[0] - ci * pair[1], cr * pair[1] + ci * pair[0])


def add_pair(a, b):
    return b if a is None else (a[0] + b[0], a[1] + b[1])


def gather_entries(coef, recv, count, chain):
    first = second = None
    for e in range(count):
        pair = (recv[e][2 * chain : 2 * chain + 1, :], recv[e][2 * chain + 1 : 2 * chain + 2, :])
        first = add_pair(first, weigh(coef, e, 4, pair))
        second = add_pair(second, weigh(coef, e, 6, pair))
    return first, second


def write_pieces(coef, pieces, count, chain, f_pair, b_pair):
    for e in range(count):
        out = add_pair(weigh(coef, e, 0, f_pair), weigh(coef, e, 2, b_pair))
        pieces[e][2 * chain : 2 * chain + 1, :] = out[0]
        pieces[e][2 * chain + 1 : 2 * chain + 2, :] = out[1]


def put_turned(t_hi, t_lo, chain, a, b, pair):
    for part in range(2):
        hi, lo = halves(pair[part])
        t_hi[chain, a, b * W : (b + 1) * W, part * W : (part + 1) * W] = hi
        t_lo[chain, a, b * W : (b + 1) * W, part * W : (part + 1) * W] = lo


def add_states(acc, t_hi, t_lo, st, a, b):
    rows = slice(b * W, (b + 1) * W)
    high = jnp.concatenate([t_hi[0, a, rows, :], t_hi[1, a, rows, :]], axis=0)
    low = jnp.concatenate([t_lo[0, a, rows, :], t_lo[1, a, rows, :]], axis=0)
    part = nn(jnp.concatenate([high, low], axis=1), st[b])
    return part if acc is None else acc + part


def put_states(acc, coef_y, y_state, y_pieces, nby, county, a):
    half = acc.shape[1] // 2
    rows = y_state.shape[2]
    turned = acc.T
    both = turned[:rows] + turned[half : half + rows]
    d = 4 * nby
    for chain in range(2):
        total = both[:, chain * W : (chain + 1) * W]
        y_state[chain, a] = total
        places = [ref.at[:, a * W : (a + 1) * W] for ref in y_pieces]
        write_pieces(
            coef_y, places, county, chain,
            (total[d : d + 1], total[d + 1 : d + 2]), (total[d + 2 : d + 3], total[d + 3 : d + 4]),
        )


def first_kernel(nby, county, src, rec, idx, table, st, coef_y, early, t_hi, t_lo, y_state, *y_pieces):
    acc = None
    for b in range(nby):
        lanes = slice(b * W, (b + 1) * W)
        put_turned(t_hi, t_lo, 0, 0, b, (src[0, 0, :, lanes], src[1, 0, :, lanes]))
        index = idx[0, :, lanes]
        cos, sin = lookup(table[0], index), lookup(table[1], index)
        put_turned(t_hi, t_lo, 1, 0, b, complex_mul((rec[0, 0, :, lanes], -rec[1, 0, :, lanes]), (cos, sin)))
        acc = add_states(acc, t_hi, t_lo, st, 0, b)
    put_states(acc, coef_y, y_state, y_pieces, nby, county, 0)


def local_kernel(nbx, nby, levels, t_hi, t_lo, y_state, my3, sp_y, lx, *refs):
    count = len(levels)
    far, (w_out, x_state), near = refs[:count], refs[count : count + 2], refs[count + 2 : 2 * count + 2]
    vx_hi, vx_lo, sems = refs[2 * count + 2 :]
    copies = []
    for n, level in enumerate(levels):
        source = far[n] if level is None else far[n].at[level]
        copies.append(pltpu.make_async_copy(source, near[n], sems.at[n]))
        copies[-1].start()
    x_state[...] = jnp.zeros_like(x_state)

    def block(i, carry):
        c, a = i // nbx, i % nbx
        state = y_state[c, a]
        for j in range(0, nby, 2):
            rows = slice(j * W, (j + 2) * W)
            high, low = t_hi[c, a, rows, :], t_lo[c, a, rows, :]
            main = nn(jnp.concatenate([high, low, high], axis=1), my3[...])
            for b in (j, j + 1):
                v = main[(b - j) * W : (b - j + 1) * W] + tn(split3(state[4 * b : 4 * b + 4, :], True), sp_y[...])
                hi, lo = halves(v)
                for part in range(2):
                    at = slice(part * W, (part + 1) * W)
                    vx_hi[at, b * W : (b + 1) * W] = hi[:, at]
                    vx_lo[at, b * W : (b + 1) * W] = lo[:, at]
        left = lx[a]
        for j in range(0, nby, 2):
            lanes = slice(j * W, (j + 2) * W)
            high, low = vx_hi[:, lanes], vx_lo[:, lanes]
            out = nn(left, jnp.concatenate([high, low, high], axis=0))
            w_out[c, a, :, lanes] = out[: 2 * W]
            x_state[c, :, lanes] += out[2 * W :]
        return carry

    lax.fori_loop(0, 2 * nbx, block, 0)
    for copy in copies:
        copy.wait()


def link_kernel(nbx, county, countx, x_local, coef_y, coef_x, sx3, edge, my3, *refs):
    recv_y, (x_state, ym), x_pieces = refs[:county], refs[county : county + 2], refs[county + 2 :]
    cols = []
    for chain in range(2):
        (fr, fi), (br, bi) = gather_entries(coef_y, recv_y, county, chain)
        rows = [(fr, fi), (-fi, fr), (br, bi), (-bi, br)]
        for a in range(nbx):
            lanes = slice(a * W, (a + 1) * W)
            cols.append(jnp.concatenate([jnp.concatenate([p[:, lanes], q[:, lanes]], axis=1) for p, q in rows]
                                        + [jnp.zeros((4, 2 * W), F32)], axis=0))
    hi, lo = halves(jnp.concatenate(cols, axis=0))
    swept = nn(jnp.concatenate([hi, lo, hi], axis=1), my3[...])
    for chain in range(2):
        for a in range(nbx):
            at = 8 * (chain * nbx + a)
            ym[chain, :, 2 * W * a : 2 * W * (a + 1)] = swept[at : at + 8]
    lines = jnp.concatenate(
        [jnp.concatenate(cols[chain * nbx : (chain + 1) * nbx], axis=1) for chain in range(2)], axis=0
    )
    hi, lo = halves(lines)
    gains = nt(sx3[...], jnp.concatenate([hi, lo, hi], axis=1))
    for chain in range(2):
        total = x_local[chain]
        for s in range(4):
            total = total + gains[:, 8 * chain + s : 8 * chain + s + 1] * edge[s : s + 1, :]
        for a in range(nbx):
            x_state[chain, a, 0:4, :] = total[4 * a : 4 * a + 4, :]
            x_state[chain, a, 4:8, :] = jnp.zeros((4, total.shape[1]), F32)
        d = 4 * nbx
        write_pieces(
            coef_x, x_pieces, countx, chain,
            (total[d : d + 1], total[d + 1 : d + 2]), (total[d + 2 : d + 3], total[d + 3 : d + 4]),
        )


def post_kernel(plan, nbx, nby, county, countx, *refs):
    refs = list(refs)
    take = lambda: refs.pop(0)
    w_in, x_state, ym, coef_x, edge, sp_x, sp_dev, table = (take() for _ in range(8))
    recv_x = [take() for _ in range(countx)]
    idx_s = take()
    idx_r, st, coef_y = (take(), take(), take()) if plan["turn"] else (None,) * 3
    olds = [{"s": (take(), take()) if z[1] == "split" else take() if z[1] == "field" else None,
             "r": take() if z[2] else None} for z in plan["images"]]
    if plan["alias"]:
        take()
    if plan["turn"]:
        t_hi, t_lo, y_state = (take() for _ in range(3))
        y_pieces = [take() for _ in range(county)]
    else:
        src_out, rec_out = take(), take()
    keep_out = take() if plan["keep"] else None
    image = take() if plan["images"] else None
    src_part, rec_part = (None, None) if plan["turn"] else (take(), take())
    keep_part = take() if plan["keep"] else None
    image_part = take() if plan["images"] else None
    sems = take()
    copies = []

    def send(part, out):
        copies.append(pltpu.make_async_copy(part, out, sems.at[len(copies)]))
        copies[-1].start()

    entries = [gather_entries(coef_x, recv_x, countx, chain) for chain in range(2)]
    step = 2 if nby % 2 == 0 else 1
    chunks = [(a, b) for a in range(nbx) for b in range(0, nby, step)]
    stacks = {}

    def correction(a, start):
        if a not in stacks:
            stacks[a] = []
            for chain in range(2):
                first, second = entries[chain]
                right = jnp.concatenate([x_state[chain, a, 0:4, :], *first, *second, edge[0:4, :]], axis=0)
                left = jnp.concatenate(
                    [sp_x[...], sp_dev[a], ym[chain, 0:4, 2 * W * a : 2 * W * (a + 1)]], axis=0
                )
                stacks[a].append((split3(left, True), split3(right, False)))
        return [tn(left, right[:, start * W : (start + step) * W]) for left, right in stacks[a]]

    def finish(a, b):
        nonlocal acc
        if plan["turn"]:
            acc = add_states(acc if b else None, t_hi, t_lo, st, a, b)
            if b == nby - 1:
                put_states(acc, coef_y, y_state, y_pieces, nby, county, a)

    acc, before = None, None
    coming = correction(*chunks[0])
    for n_chunk, (a, start) in enumerate(chunks):
        place = slice(a * W, (a + 1) * W)
        fixes = coming
        if n_chunk + 1 < len(chunks):
            coming = correction(*chunks[n_chunk + 1])
        for b in range(start, start + step):
            lanes = slice(b * W, (b + 1) * W)
            fields = []
            for chain in range(2):
                u = w_in[chain, a, :, lanes] + fixes[chain][:, (b - start) * W : (b - start + 1) * W]
                fields.append((u[:W], u[W:]))
            index = idx_s[place, lanes]
            source = complex_mul(fields[0], (lookup(table[0], index), lookup(table[1], index)))
            back = fields[1]
            if plan["turn"]:
                put_turned(t_hi, t_lo, 0, a, b, source)
                index = idx_r[place, lanes]
                turn = (lookup(table[0], index), lookup(table[1], index))
                put_turned(t_hi, t_lo, 1, a, b, complex_mul(back, turn))
            else:
                src_part[a, 0, :, lanes], src_part[a, 1, :, lanes] = source
                rec_part[a, 0, :, lanes], rec_part[a, 1, :, lanes] = back[0], -back[1]
            if keep_out is not None:
                keep_part[a, 0, :, lanes], keep_part[a, 1, :, lanes] = back
            for n, (old, (_, how, has_r)) in enumerate(zip(olds, plan["images"])):
                if how == "split":
                    hi, lo = old["s"]
                    rows = slice(b * W, (b + 1) * W)
                    s = [hi[a, rows, p * W : (p + 1) * W].astype(F32) + lo[a, rows, p * W : (p + 1) * W].astype(F32)
                         for p in range(2)]
                elif how == "field":
                    s = (old["s"][0, 0, place, lanes], old["s"][1, 0, place, lanes])
                else:
                    s = source
                r = (old["r"][0, place, lanes], old["r"][1, place, lanes]) if has_r else back
                image_part[n, a, :, lanes] = s[0] * r[0] - s[1] * r[1]
            if before is not None:
                finish(*before)
            before = (a, b)
        if start + step < nby:
            continue
        if not plan["turn"]:
            send(src_part.at[a], src_out.at[:, 0, place])
            send(rec_part.at[a], rec_out.at[:, 0, place])
        if plan["keep"]:
            send(keep_part.at[a], keep_out.at[:, place])
        for n, (z, _, _) in enumerate(plan["images"]):
            send(image_part.at[n, a], image.at[z, place])
    finish(*before)
    for copy in copies:
        copy.wait()


def whole(shape):
    return pl.BlockSpec(shape, lambda *_: (0,) * len(shape))


SMEM = pl.BlockSpec(memory_space=pltpu.SMEM)
VMEM = pl.BlockSpec(memory_space=pltpu.VMEM)
ANY = pl.BlockSpec(memory_space=pl.ANY)


def in_hbm(x):
    return pltpu.with_memory_space_constraint(x, pltpu.HBM)


def params(mib):
    return pltpu.CompilerParams(vmem_limit_bytes=mib * MIB)


def on_device(source_field, receiver_field, velocity_index, slowness, freq_index, root_modulus, root_angle):
    depth, len_x, len_y = velocity_index.shape
    nbx, nby = len_x // W, len_y // W
    countx, county = lax.axis_size("gx"), lax.axis_size("gy")
    modulus, angle = root_modulus[0], root_angle[0]
    diag, off, end = sweep_factors(modulus, angle)

    entries = slowness.shape[0]
    chunks = -(-entries // W)
    rate = freq_index.astype(F32)[0] * PHASE_UNIT
    phase = jnp.pad(rate * slowness, (0, chunks * W - entries)).reshape(chunks, W)
    table = jnp.stack([jnp.cos(phase), jnp.sin(phase)])

    at = np.arange(W)
    dist = np.abs(at[:, None] - at[None, :]).astype(np.int32)
    pw = root_powers(modulus, angle, jnp.asarray(dist))
    pw = complex_mul(off, pw)
    on = jnp.asarray(dist == 0)
    mr, mi = jnp.where(on, diag[0], pw[0]), jnp.where(on, diag[1], pw[1])
    my = jnp.concatenate([jnp.concatenate([mr, mi], 1), jnp.concatenate([-mi, mr], 1)], 0)
    mx = jnp.concatenate([jnp.concatenate([mr, -mi], 1), jnp.concatenate([mi, mr], 1)], 0)
    my_hi, my_lo = rounded_halves(my)
    mx_hi, mx_lo = rounded_halves(mx)

    rows_y = -(-(4 * nby + 4) // 16) * 16
    rows_x = -(-(4 * nbx + 4) // 16) * 16
    st_hi, st_lo = rounded_halves(pad_rows(state_matrix(modulus, angle, len_y), -(-rows_y // 64) * 64))
    st = jnp.concatenate([jnp.concatenate([st_hi, st_lo], axis=0), jnp.concatenate([st_hi, 0 * st_lo], axis=0)], axis=1)
    st = st.reshape(st.shape[0], 2, nby, 2 * W).transpose(2, 1, 3, 0).reshape(nby, 4 * W, st.shape[0])
    sx = pad_rows(state_matrix(modulus, angle, len_x), rows_x)
    sx_hi, sx_lo = rounded_halves(sx)
    lx = jnp.concatenate([
        jnp.broadcast_to(jnp.concatenate([mx_hi, mx_hi, mx_lo], axis=1)[None], (nbx, 2 * W, 6 * W)),
        jnp.concatenate([x.reshape(rows_x, nbx, 2 * W).transpose(1, 0, 2) for x in (sx_hi, sx_hi, sx_lo)], axis=2),
    ], axis=1)
    my3 = jnp.concatenate([my_hi, my_hi, my_lo], axis=0)

    near = complex_mul(off, root_powers(modulus, angle, jnp.asarray(np.stack([at + 1, W - at]).astype(np.int32))))
    spread = spread_rows(near)
    sp_hi, sp_lo = rounded_halves(spread)
    sp_y = jnp.concatenate([sp_hi, sp_hi, sp_lo], axis=0)

    def edges(length):
        m = np.arange(length)
        ahead = complex_mul(off, root_powers(modulus, angle, jnp.asarray((m + 1).astype(np.int32))))
        behind = root_powers(modulus, angle, jnp.asarray((length - 1 - m).astype(np.int32)))
        return jnp.stack([ahead[0], behind[0]]), jnp.stack([ahead[1], behind[1]])

    edge_x = spread_rows(edges(len_x)).reshape(4, nbx, 2 * W).transpose(1, 0, 2)
    er, ei = edges(len_y)
    edge_y = jnp.concatenate([jnp.stack([er, ei], axis=1).reshape(4, len_y), jnp.zeros((4, len_y), F32)], axis=0)

    coef_y = link_coefs(modulus, angle, off, end, county, lax.axis_index("gy"), len_y)
    coef_x = link_coefs(modulus, angle, off, end, countx, lax.axis_index("gx"), len_x)

    sx3 = jnp.concatenate([sx_hi, sx_hi, sx_lo], axis=1)
    (my3, sp_y, lx, sx3, edge_y, spread, edge_x, table, st, coef_y, coef_x) = lax.optimization_barrier(
        (my3, sp_y, lx, sx3, edge_y, spread, edge_x, table, st, coef_y, coef_x)
    )

    turned = jax.ShapeDtypeStruct((2, nbx, nby * W, 2 * W), BF16)
    turned_spec = pl.BlockSpec((2, 1, nby * W, 2 * W), lambda a: (0, a, 0, 0))
    y_state_shape = jax.ShapeDtypeStruct((2, nbx, rows_y, W), F32)
    y_state_spec = pl.BlockSpec((2, 1, rows_y, W), lambda a: (0, a, 0, 0))
    y_piece_shape = jax.ShapeDtypeStruct((4, len_x), F32)
    y_piece_spec = pl.BlockSpec((4, W), lambda a: (0, a))
    field_spec = pl.BlockSpec((2, 1, W, len_y), lambda a: (0, 0, a, 0))
    level_spec = lambda z: pl.BlockSpec((1, W, len_y), lambda a: (z, a, 0))
    turn_out = [turned, turned, y_state_shape] + [y_piece_shape] * county
    turn_specs = [turned_spec, turned_spec, y_state_spec] + [y_piece_spec] * county

    t_hi, t_lo, y_state, *y_pieces = pl.pallas_call(
        functools.partial(first_kernel, nby, county),
        grid=(nbx,),
        in_specs=[field_spec, field_spec, level_spec(depth - 1), whole(table.shape), whole(st.shape), SMEM, ANY],
        out_specs=turn_specs,
        out_shape=turn_out,
        compiler_params=params(20),
        name="first",
    )(in_hbm(source_field), in_hbm(receiver_field), in_hbm(velocity_index), table, st, coef_y, my3)

    def local(t_hi, t_lo, y_state, ahead):
        shapes = [x.shape if level is None else x.shape[1:] for x, level in ahead]
        return pl.pallas_call(
            functools.partial(local_kernel, nbx, nby, tuple(level for _, level in ahead)),
            in_specs=[VMEM] * 6 + [ANY] * len(ahead),
            out_specs=[VMEM] * (2 + len(ahead)),
            out_shape=[
                jax.ShapeDtypeStruct((2, nbx, 2 * W, len_y), F32),
                jax.ShapeDtypeStruct((2, rows_x, len_y), F32),
            ] + [jax.ShapeDtypeStruct(shape, x.dtype) for (x, _), shape in zip(ahead, shapes)],
            scratch_shapes=[pltpu.VMEM((2 * W, len_y), BF16)] * 2 + [pltpu.SemaphoreType.DMA((len(ahead),))],
            compiler_params=params(8),
            name="local",
        )(t_hi, t_lo, y_state, my3, sp_y, lx, *[in_hbm(x) for x, _ in ahead])

    link = pl.pallas_call(
        functools.partial(link_kernel, nbx, county, countx),
        in_specs=[VMEM] + [SMEM] * 2 + [VMEM] * (3 + county),
        out_specs=[VMEM] * (2 + countx),
        out_shape=[
            jax.ShapeDtypeStruct((2, nbx, 8, len_y), F32),
            jax.ShapeDtypeStruct((2, 8, 2 * len_x), F32),
        ] + [jax.ShapeDtypeStruct((4, len_y), F32)] * countx,
        compiler_params=params(8),
        name="link",
    )

    source_levels = {0: ("field", (source_field,))}
    kept = {}
    image = None
    for step in range(depth):
        turn = step < depth - 1
        level_r = depth - 1 - step
        todo = [z for z in range(depth) if max(z - 1, depth - 1 - z) == step]
        plan = {
            "turn": turn,
            "keep": level_r - 1 > step,
            "images": [(z, None if z - 1 == step else source_levels[z][0], z != level_r) for z in todo],
            "alias": bool(todo) and image is not None,
        }
        ahead = [(velocity_index, step)] + ([(velocity_index, depth - 2 - step)] if turn else [])
        for z, how, has_r in plan["images"]:
            if how == "split":
                ahead += [(x, 0) for x in source_levels[z][1]]
            elif how == "field":
                ahead += [(x, None) for x in source_levels[z][1]]
            if has_r:
                ahead += [(kept[z], None)]
        w, x_local, *fetched = local(t_hi, t_lo, y_state, ahead)
        recv_y = exchange(y_pieces, "gy")
        x_state, ym, *x_pieces = link(x_local, coef_y, coef_x, sx3, edge_y, my3, *recv_y)
        recv_x = exchange(x_pieces, "gx")
        args = [w, x_state, ym, coef_x, edge_y, spread, edge_x, table, *recv_x, fetched.pop(0)]
        specs = [VMEM] * 3 + [SMEM] + [VMEM] * (5 + countx)
        if turn:
            args += [fetched.pop(0), st, coef_y]
            specs += [VMEM, VMEM, SMEM]
        args += fetched
        specs += [VMEM] * len(fetched)
        aliases, scratch, sends = {}, [], 0
        if turn:
            shapes, out_specs = list(turn_out), [VMEM] * len(turn_out)
        else:
            shapes = [pltpu.HBM(source_field.shape, F32)] * 2
            out_specs = [ANY] * 2
            scratch += [pltpu.VMEM((nbx, 2, W, len_y), F32)] * 2
            sends += 2
        if plan["keep"]:
            shapes.append(pltpu.HBM((2, len_x, len_y), F32))
            out_specs.append(ANY)
            scratch += [pltpu.VMEM((nbx, 2, W, len_y), F32)]
            sends += 1
        if todo:
            if plan["alias"]:
                aliases = {len(args): len(shapes)}
                args += [in_hbm(image)]
                specs += [ANY]
            shapes.append(pltpu.HBM((depth, len_x, len_y), F32))
            out_specs.append(ANY)
            scratch += [pltpu.VMEM((len(todo), nbx, W, len_y), F32)]
            sends += len(todo)
        outs = pl.pallas_call(
            functools.partial(post_kernel, plan, nbx, nby, county, countx),
            in_specs=specs,
            out_specs=out_specs,
            out_shape=shapes,
            scratch_shapes=scratch + [pltpu.SemaphoreType.DMA((max(sends, 1) * nbx,))],
            input_output_aliases=aliases,
            compiler_params=params(20),
            name="post",
        )(*args)
        outs = list(outs)
        if turn:
            t_hi, t_lo, y_state, *y_pieces = outs[: 3 + county]
            outs = outs[3 + county :]
            source_levels[step + 1] = ("split", (t_hi, t_lo))
        else:
            source, receiver = outs[:2]
            outs = outs[2:]
        if plan["keep"]:
            kept[level_r] = outs.pop(0)
        if todo:
            image = outs.pop(0)
    return image, source, receiver


def solution(mesh):
    placed = (
        P(None, None, "gx", "gy"),
        P(None, None, "gx", "gy"),
        P(None, "gx", "gy"),
        P(),
        P(),
        P(),
        P(),
    )
    return jax.shard_map(
        on_device,
        mesh=mesh,
        in_specs=placed,
        out_specs=(P(None, "gx", "gy"), P(None, None, "gx", "gy"), P(None, None, "gx", "gy")),
        check_vma=False,
    )
```
